256 devices in a mesh: dp: 4 (over y), row: 8 (over x, core), col: 8 (over z).
Axes of the slice: x: 4, y: 4, z: 8, core: 2. Of those that a mesh axis runs over, the one named last changes fastest.
Arguments:
- grad_parts: bfloat16 [4, 4096, 14336], P('dp', 'row', 'col'), may hold values from -3 to 3
- momentum: bfloat16 [4096, 14336], P(('row', 'dp'), 'col'), may hold values from -96 to 96
- right_prev: bfloat16 [14336, 128], P('col'), may hold values from -0.046875 to 0.046875
Outputs:
- momentum_next: bfloat16 [4096, 14336], P(('row', 'dp'), 'col')
- right_next: bfloat16 [14336, 128], P('col')
- update: bfloat16 [4096, 14336], P(('row', 'dp'), 'col')
The draws below stay inside these ranges and needn't reach their ends.
All inputs are finite; a program needn't handle non-finite values.
Results may differ from the reference program's by a relative error of at most 0.024.
Values may be sent and summed in bfloat16 or wider, within the bound.
A program may use at most 64 MiB of HBM per device.

```python
import math
import jax
import jax.numpy as jnp
from jax import lax

COLS = 14336
RANK = 128
ITERS = 2
ROWS = 4096
COL_DEV = 1792
N_DP = 4


def draw_momentum(key, part):
    key = jax.random.fold_in(key, 11)
    k_base, k_rows, k_cols = jax.random.split(key, 3)
    base = jnp.clip(jax.random.normal(k_base, (ROWS, COLS), jnp.float32), -4.0, 4.0)
    rise = math.log(4.0)
    row_scale = jnp.exp(jax.random.uniform(k_rows, (ROWS, 1), jnp.float32, math.log(0.3), math.log(3.0)))
    col_random = jnp.exp(jax.random.uniform(k_cols, (1, COLS), jnp.float32, math.log(0.5), math.log(2.0)))
    position = (jnp.arange(COLS, dtype=jnp.int32) % COL_DEV).astype(jnp.float32) / COL_DEV
    col_scale = col_random * jnp.exp(rise * position)[None, :]
    return (base * row_scale * col_scale).astype(jnp.bfloat16)


def levels(key, dims, pieces, low, high):
    level, own = 1.0, jax.random.fold_in(key, 6)
    for dim, parts in pieces:
        heights = jnp.exp(jax.random.uniform(jax.random.fold_in(own, dim), (parts,), jnp.float32, low / len(pieces), high / len(pieces)))
        level = level * jnp.repeat(heights, dims[dim] // parts).reshape([-1 if axis == dim else 1 for axis in range(len(dims))])
    return level


def gaussian(own_key, dims, spread, reach, cuts=(), held_as=jnp.bfloat16):
    gain = levels(own_key, dims, cuts, -0.22, 0.18) if cuts else 1.0
    values = jax.random.normal(own_key, dims, jnp.float32) * spread * gain
    return jnp.minimum(jnp.maximum(values, -reach), reach).astype(held_as)


def setup_inputs(seed: int = 0) -> dict:
    streams_of = jax.random.split(jax.random.key(seed), 4)
    grad_parts = gaussian(streams_of[0], (N_DP, ROWS, COLS), 0.5, 3.0, ((0, 4), (1, 8), (2, 8)))
    momentum = draw_momentum(jax.random.fold_in(streams_of[3], 71), 0)
    right_prev = gaussian(streams_of[2], (COLS, RANK), COLS ** -0.5, 0.046875, ((0, 8),))
    return {"grad_parts": grad_parts, "momentum": momentum, "right_prev": right_prev}


def reference(grad_parts, momentum, right_prev):
    grad_sum = lax.optimization_barrier(jnp.sum(grad_parts.astype(jnp.float32), axis=0))
    buffer = (momentum.astype(jnp.float32) + grad_sum).astype(jnp.bfloat16)
    right = right_prev
    for step in range(ITERS):
        power = jnp.dot(buffer.astype(jnp.float32), right.astype(jnp.float32), preferred_element_type=jnp.float32)
        gram = jnp.dot(power.T, power, precision=lax.Precision.HIGHEST)
        lower = jnp.linalg.cholesky(gram)
        basis = jax.scipy.linalg.solve_triangular(lower, power.T, lower=True).T.astype(jnp.bfloat16)
        back = jnp.dot(buffer.T.astype(jnp.float32), basis.astype(jnp.float32), preferred_element_type=jnp.float32)
        scale = lax.rsqrt(lax.optimization_barrier(jnp.sum(back * back, axis=0)) + 1e-06)
        right = (back * scale).astype(jnp.bfloat16)
    back_half = back.astype(jnp.bfloat16)
    correction = jnp.dot(basis.astype(jnp.float32), back_half.T.astype(jnp.float32), preferred_element_type=jnp.float32)
    momentum_next = (buffer.astype(jnp.float32) - 0.25 * correction).astype(jnp.bfloat16)
    factor = math.sqrt(ROWS * COLS / RANK)
    update = (factor * jnp.dot(basis.astype(jnp.float32), right.T.astype(jnp.float32), preferred_element_type=jnp.float32)).astype(jnp.bfloat16)
    return (momentum_next, right, update)
```

```python
import functools
import math

import jax
import jax.numpy as jnp
from jax import lax
from jax.experimental import pallas as pl
from jax.experimental.pallas import tpu as pltpu
from jax.sharding import PartitionSpec as P

f32 = jnp.float32
bf16 = jnp.bfloat16
HIGHEST = lax.Precision.HIGHEST
MESH = pl.DeviceIdType.MESH
RANK = 128
ROWS_DEV = 128
PANEL = 8


def nt(a, b, precision=None):
    return lax.dot_general(a, b, (((1,), (1,)), ((), ())), precision=precision, preferred_element_type=f32)


def nn(a, b, precision=None):
    return lax.dot_general(a, b, (((1,), (0,)), ((), ())), precision=precision, preferred_element_type=f32)


def halves(x):
    high = x.astype(bf16)
    return high, (x - high.astype(f32)).astype(bf16)


def nn3(a, b):
    a_high, a_low = halves(a)
    b_high, b_low = halves(b)
    return nn(a_high, b_high) + (nn(a_high, b_low) + nn(a_low, b_high))


def inverse_cholesky(a, ahead=2):
    n, count = RANK, RANK // PANEL
    rows = [a[PANEL * i : PANEL * (i + 1), :] for i in range(count)]
    row = lax.broadcasted_iota(jnp.int32, (PANEL, n), 0)
    lane = lax.broadcasted_iota(jnp.int32, (PANEL, n), 1)
    inv = [(lane == row + PANEL * i).astype(f32) for i in range(count)]
    out = []
    for b in range(count):
        end = min(count, b + 1 + ahead)
        cols = [
            [jnp.broadcast_to(rows[i][:, PANEL * b + k : PANEL * b + k + 1], (PANEL, n)) for k in range(PANEL)]
            for i in range(b, end)
        ]
        recips = []
        for j in range(PANEL):
            recip = 1.0 / jnp.broadcast_to(cols[0][j][j : j + 1, :], (PANEL, n))
            recips.append(recip)
            pivots = [jnp.broadcast_to(cols[0][k][j : j + 1, :], (PANEL, n)) for k in range(j + 1, PANEL)]
            row_a = jnp.broadcast_to(rows[b][j : j + 1, :], (PANEL, n))
            row_w = jnp.broadcast_to(inv[b][j : j + 1, :], (PANEL, n))
            for i in range(b, end):
                m = cols[i - b][j] * recip
                if i == b:
                    m = jnp.where(row > j, m, 0.0)
                for k in range(j + 1, PANEL):
                    cols[i - b][k] = cols[i - b][k] - m * pivots[k - j - 1]
                rows[i] = rows[i] - m * row_a
                inv[i] = inv[i] - m * row_w
        scale = recips[0]
        for j in range(1, PANEL):
            scale = jnp.where(row == j, recips[j], scale)
        out.append(inv[b] * jnp.sqrt(scale))
        if end < count:
            left = jnp.transpose(rows[b] * scale)[PANEL * end :, :]
            update = nn(left, jnp.concatenate([rows[b], inv[b]], 1), HIGHEST)
            for i in range(end, count):
                part = update[PANEL * (i - end) : PANEL * (i - end + 1), :]
                rows[i] = rows[i] - part[:, :n]
                inv[i] = inv[i] - part[:, n:]
    return jnp.concatenate(out, 0)


def column(row):
    return jnp.transpose(jnp.broadcast_to(row, (RANK, RANK)))


def kernel(
    ny, nx, nz, cols, factor,
    grads, mom_hbm, right_hbm,
    mom_out, right_out, upd_out,
    g_all, g_recv, mom, right0, buf2,
    p1_part, p1_recv, zbuf, z_part, z_recv,
    m_send, m_recv, m_own, m_slots, m_full, m_other,
    g_part, g_core, g_slots, g_full,
    n_mine, n1_recv, n2_recv, back_own, back_other,
    local_sem, send, recv,
):
    half = cols // 2
    chips = ny * nx
    zr = RANK // nz
    cr = RANK // chips
    y = lax.axis_index("dp")
    r = lax.axis_index("row")
    z = lax.axis_index("col")
    x = r // 2
    c = lax.rem(r, 2)

    def dev(dy=0, dx=0, dc=0, dz=0):
        return {
            "dp": lax.rem(y + dy, ny),
            "row": lax.rem(x + dx, nx) * 2 + lax.rem(c + dc, 2),
            "col": lax.rem(z + dz, nz),
        }

    yz = [(dy, dz) for dz in range(nz) for dy in range(ny) if dy or dz]
    plane = [(dy, dx) for dy in range(ny) for dx in range(nx) if dy or dx]
    zc = [(dz, dc) for dz in range(nz) for dc in range(2) if dz or dc]

    met = []
    for dy, dz in yz:
        met.append((dy, 0, 0, dz))
    for dy, dx in plane:
        if (dy, dx, 0, 0) not in met:
            met.append((dy, dx, 0, 0))
    for dz, dc in zc:
        if (0, 0, dc, dz) not in met:
            met.append((0, 0, dc, dz))
    barrier = pltpu.get_barrier_semaphore()
    for offsets in met:
        pl.semaphore_signal(barrier, inc=1, device_id=dev(*offsets), device_id_type=MESH)

    loads = []
    for i, (src, dst) in enumerate([(right_hbm, right0), (grads.at[0], g_all), (mom_hbm, mom)]):
        copy = pltpu.make_async_copy(src, dst, local_sem.at[i])
        copy.start()
        loads.append(copy)
    sent = []

    def put(src, dst, slot, target):
        pltpu.make_async_remote_copy(
            src_ref=src, dst_ref=dst, send_sem=send.at[slot], recv_sem=recv.at[slot],
            device_id=target, device_id_type=MESH,
        ).start()

    def landed(ref, slot):
        copy = pltpu.make_async_remote_copy(
            src_ref=ref, dst_ref=ref, send_sem=send.at[slot], recv_sem=recv.at[slot],
            device_id=dev(), device_id_type=MESH,
        )
        copy.wait_recv()
        sent.append(copy)

    pl.semaphore_wait(barrier, len(met))

    for dy in range(1, ny):
        there = lax.rem(y + dy, ny)
        put(grads.at[0, pl.ds(pl.multiple_of(there * ROWS_DEV, ROWS_DEV), ROWS_DEV), :], g_recv.at[dy - 1], 0, dev(dy))

    loads[0].wait()
    right_t = jnp.transpose(right0[...])
    loads[1].wait()
    for i in range(ny):
        p1_part[i] = nt(right_t, g_all[pl.ds(i * ROWS_DEV, ROWS_DEV), :])
    loads[2].wait()
    p1_part[y] = p1_part[y] + nt(right_t, mom[...])
    for i, (dy, dz) in enumerate(yz):
        there_y, there_z = lax.rem(y + dy, ny), lax.rem(z + dz, nz)
        put(p1_part.at[there_y, pl.ds(pl.multiple_of(there_z * zr, zr), zr), :], p1_recv.at[i], 1, dev(dy, 0, 0, dz))
    z_rows = pl.ds(pl.multiple_of(z * zr, zr), zr)

    def gather_z(step, slot):
        for dz in range(1, nz):
            put(zbuf.at[step, z_rows, :], zbuf.at[step, z_rows, :], slot, dev(0, 0, 0, dz))

    landed(p1_recv, 1)
    total = p1_part[y, z_rows, :]
    for i in range(len(yz)):
        total = total + p1_recv[i]
    zbuf[0, z_rows, :] = total
    gather_z(0, 2)

    landed(g_recv, 0)
    summed = g_all[pl.ds(pl.multiple_of(y * ROWS_DEV, ROWS_DEV), ROWS_DEV), :].astype(f32)
    for i in range(ny - 1):
        summed = summed + g_recv[i].astype(f32)
    buffer = (mom[...].astype(f32) + summed).astype(bf16)
    buf2[0:ROWS_DEV, :] = buffer
    buf2[ROWS_DEV:, :] = buffer

    mine = pl.ds(pl.multiple_of(c * half, 128), half)
    others = pl.ds(pl.multiple_of((1 - c) * half, 128), half)
    here = y * nx + x
    chip_rows = pl.ds(pl.multiple_of(here * cr, cr), cr)

    def reduce_plane(step, power):
        slot = 3 + 8 * step
        g_part[step] = nt(power, power, HIGHEST)
        put(g_part.at[step], g_core.at[step], slot, dev(0, 0, 1))
        both = jnp.concatenate(halves(power), 1)
        m_send[step] = nn(both, buf2[:, others])
        put(m_send.at[step], m_recv.at[step], slot + 1, dev(0, 0, 1))
        m_own[step] = nn(both, buf2[:, mine])
        landed(g_core.at[step], slot)
        g_part_sum = g_part[step] + g_core[step]
        g_core[step] = g_part_sum
        for i, (dy, dx) in enumerate(plane):
            there = lax.rem(y + dy, ny) * nx + lax.rem(x + dx, nx)
            rows = pl.ds(pl.multiple_of(there * cr, cr), cr)
            put(g_core.at[step, rows, :], g_slots.at[step, i], slot + 2, dev(dy, dx))
        landed(m_recv.at[step], slot + 1)
        m_own[step] = m_own[step] + m_recv[step]
        for i, (dy, dx) in enumerate(plane):
            there = lax.rem(y + dy, ny) * nx + lax.rem(x + dx, nx)
            rows = pl.ds(pl.multiple_of(there * cr, cr), cr)
            put(m_own.at[step, rows, :], m_slots.at[step, i], slot + 3, dev(dy, dx))
        landed(g_slots.at[step], slot + 2)
        total = g_core[step, chip_rows, :]
        for i in range(len(plane)):
            total = total + g_slots[step, i]
        g_full[step, chip_rows, :] = total
        for dy, dx in plane:
            put(g_full.at[step, chip_rows, :], g_full.at[step, chip_rows, :], slot + 4, dev(dy, dx))
        landed(m_slots.at[step], slot + 3)
        total = m_own[step, chip_rows, :]
        for i in range(len(plane)):
            total = total + m_slots[step, i]
        m_full[step, chip_rows, :] = total
        for dy, dx in plane:
            put(m_full.at[step, chip_rows, :], m_full.at[step, chip_rows, :], slot + 5, dev(dy, dx))

    def gram_done(step):
        landed(g_slots.at[step], 3 + 8 * step + 4)
        return g_full[step]

    def back_done(step):
        landed(m_slots.at[step], 3 + 8 * step + 5)

    landed(z_recv, 2)
    reduce_plane(0, zbuf[0])
    back_done(0)
    put(m_full.at[0], m_other, 9, dev(0, 0, 1))
    both = jnp.concatenate(halves(m_full[0]), 0)
    next_part = nt(both, buf2[0:ROWS_DEV, mine])
    landed(m_other, 9)
    both = jnp.concatenate(halves(m_other[...]), 0)
    next_part = next_part + nt(both, buf2[0:ROWS_DEV, others])
    z_part[...] = next_part[:RANK] + next_part[RANK:]
    for dz in range(1, nz):
        there = lax.rem(z + dz, nz)
        put(z_part.at[pl.ds(pl.multiple_of(there * zr, zr), zr), :], z_recv.at[dz - 1], 19, dev(0, 0, 0, dz))
    w1 = inverse_cholesky(gram_done(0))
    landed(z_recv, 19)
    total = z_part[z_rows, :]
    for i in range(nz - 1):
        total = total + z_recv[i]
    zbuf[1, z_rows, :] = total
    gather_z(1, 20)
    back_a = nn3(w1, m_full[0])
    back_b = nn3(w1, m_other[...])
    own_sum = jnp.sum(back_a * back_a, axis=1, keepdims=True) + jnp.sum(back_b * back_b, axis=1, keepdims=True)
    own_col = jnp.broadcast_to(own_sum, (RANK, RANK))
    own_row = jnp.transpose(own_col)
    n_mine[0] = own_row[0:8, :]
    for dz in range(1, nz):
        put(n_mine.at[0], n1_recv.at[dz - 1], 21, dev(0, 0, 0, dz))
    landed(z_recv, 20)

    power = nn(w1, zbuf[1], HIGHEST) * lax.rsqrt(own_col + 1e-6)
    reduce_plane(1, power)
    landed(n1_recv, 21)
    norm = own_row[0:1, :]
    for i in range(nz - 1):
        norm = norm + n1_recv[i, 0:1, :]
    rest = jnp.sqrt((own_row[0:1, :] + 1e-6) / (norm + 1e-6))
    gram = gram_done(1) * column(rest) * rest
    w2 = inverse_cholesky(gram) * rest
    basis = jnp.transpose(nn(w2, power, HIGHEST)).astype(bf16)
    back_done(1)
    back_own[...] = jnp.transpose(nn3(w2, m_full[1]))
    put(back_own, back_other, 22, dev(0, 0, 1))
    part = jnp.sum(back_own[...] * back_own[...], axis=0, keepdims=True)
    n_mine[1] = jnp.broadcast_to(part, (8, RANK))
    for i, (dz, dc) in enumerate(zc):
        put(n_mine.at[1], n2_recv.at[i], 23, dev(0, 0, dc, dz))
    mom_out[:, mine] = (
        buf2[0:ROWS_DEV, mine].astype(f32) - 0.25 * nt(basis, back_own[...].astype(bf16))
    ).astype(bf16)
    landed(back_other, 22)
    mom_out[:, others] = (
        buf2[0:ROWS_DEV, others].astype(f32) - 0.25 * nt(basis, back_other[...].astype(bf16))
    ).astype(bf16)
    landed(n2_recv, 23)
    norm = part
    for i in range(len(zc)):
        norm = norm + n2_recv[i, 0:1, :]
    scale = lax.rsqrt(norm + 1e-6)
    for where, back in ((mine, back_own), (others, back_other)):
        right = (back[...] * scale).astype(bf16)
        right_out[where, :] = right
        upd_out[:, where] = (factor * nt(basis, right)).astype(bf16)
    for copy in sent:
        copy.wait_send()


def solution(mesh):
    ny, nx, nz = mesh.shape["dp"], mesh.shape["row"] // 2, mesh.shape["col"]

    def on_device(grad_parts, momentum, right_prev):
        cols = momentum.shape[1]
        half, chips = cols // 2, ny * nx
        zr, cr = RANK // nz, RANK // chips
        factor = math.sqrt(ny * nx * 2 * ROWS_DEV * cols * nz / RANK)
        vmem = pltpu.VMEM
        any_space = pl.BlockSpec(memory_space=pl.ANY)
        in_vmem = pl.BlockSpec(memory_space=pltpu.VMEM)
        return pl.pallas_call(
            functools.partial(kernel, ny, nx, nz, cols, factor),
            out_shape=(
                jax.ShapeDtypeStruct((ROWS_DEV, cols), bf16),
                jax.ShapeDtypeStruct((cols, RANK), bf16),
                jax.ShapeDtypeStruct((ROWS_DEV, cols), bf16),
            ),
            in_specs=[any_space] * 3,
            out_specs=(in_vmem,) * 3,
            scratch_shapes=[
                vmem((ny * ROWS_DEV, cols), bf16),
                vmem((ny - 1, ROWS_DEV, cols), bf16),
                vmem((ROWS_DEV, cols), bf16),
                vmem((cols, RANK), bf16),
                vmem((2 * ROWS_DEV, cols), bf16),
                vmem((ny, RANK, ROWS_DEV), f32),
                vmem((ny * nz - 1, zr, ROWS_DEV), f32),
                vmem((2, RANK, ROWS_DEV), f32),
                vmem((RANK, ROWS_DEV), f32),
                vmem((nz - 1, zr, ROWS_DEV), f32),
                vmem((2, RANK, half), f32),
                vmem((2, RANK, half), f32),
                vmem((2, RANK, half), f32),
                vmem((2, chips - 1, cr, half), f32),
                vmem((2, RANK, half), f32),
                vmem((RANK, half), f32),
                vmem((2, RANK, RANK), f32),
                vmem((2, RANK, RANK), f32),
                vmem((2, chips - 1, cr, RANK), f32),
                vmem((2, RANK, RANK), f32),
                vmem((2, 8, RANK), f32),
                vmem((nz - 1, 8, RANK), f32),
                vmem((2 * nz - 1, 8, RANK), f32),
                vmem((half, RANK), f32),
                vmem((half, RANK), f32),
                pltpu.SemaphoreType.DMA((3,)),
                pltpu.SemaphoreType.DMA((24,)),
                pltpu.SemaphoreType.DMA((24,)),
            ],
            compiler_params=pltpu.CompilerParams(
                collective_id=0, has_side_effects=True, vmem_limit_bytes=48 * 1024 * 1024
            ),
            cost_estimate=pl.CostEstimate(flops=10**9, bytes_accessed=4 * 10**6, transcendentals=0),
        )(grad_parts, momentum, right_prev)

    return jax.shard_map(
        on_device,
        mesh=mesh,
        in_specs=(P("dp", "row", "col"), P(("row", "dp"), "col"), P("col", None)),
        out_specs=(P(("row", "dp"), "col"), P("col", None), P(("row", "dp"), "col")),
        check_vma=False,
    )
```

```python
import functools
import math

import jax
import jax.numpy as jnp
from jax import lax
from jax.experimental import pallas as pl
from jax.experimental.pallas import tpu as pltpu
from jax.sharding import PartitionSpec as P

f32 = jnp.float32
bf16 = jnp.bfloat16
HIGHEST = lax.Precision.HIGHEST
MESH = pl.DeviceIdType.MESH
RANK = 128
ROWS_DEV = 128
PANEL = 8


def nt(a, b, precision=None):
    return lax.dot_general(a, b, (((1,), (1,)), ((), ())), precision=precision, preferred_element_type=f32)


def nn(a, b, precision=None):
    return lax.dot_general(a, b, (((1,), (0,)), ((), ())), precision=precision, preferred_element_type=f32)


def halves(x):
    high = x.astype(bf16)
    return high, (x - high.astype(f32)).astype(bf16)


def nn3(a, b):
    a_high, a_low = halves(a)
    b_high, b_low = halves(b)
    return nn(a_high, b_high) + (nn(a_high, b_low) + nn(a_low, b_high))


def inverse_cholesky(a, ahead=2):
    n, count = RANK, RANK // PANEL
    rows = [a[PANEL * i : PANEL * (i + 1), :] for i in range(count)]
    row = lax.broadcasted_iota(jnp.int32, (PANEL, n), 0)
    lane = lax.broadcasted_iota(jnp.int32, (PANEL, n), 1)
    inv = [(lane == row + PANEL * i).astype(f32) for i in range(count)]
    out = []
    for b in range(count):
        end = min(count, b + 1 + ahead)
        cols = [
            [jnp.broadcast_to(rows[i][:, PANEL * b + k : PANEL * b + k + 1], (PANEL, n)) for k in range(PANEL)]
            for i in range(b, end)
        ]
        recips = []
        for j in range(PANEL):
            recip = 1.0 / jnp.broadcast_to(cols[0][j][j : j + 1, :], (PANEL, n))
            recips.append(recip)
            pivots = [jnp.broadcast_to(cols[0][k][j : j + 1, :], (PANEL, n)) for k in range(j + 1, PANEL)]
            row_a = jnp.broadcast_to(rows[b][j : j + 1, :], (PANEL, n))
            row_w = jnp.broadcast_to(inv[b][j : j + 1, :], (PANEL, n))
            for i in range(b, end):
                m = cols[i - b][j] * recip
                if i == b:
                    m = jnp.where(row > j, m, 0.0)
                for k in range(j + 1, PANEL):
                    cols[i - b][k] = cols[i - b][k] - m * pivots[k - j - 1]
                rows[i] = rows[i] - m * row_a
                inv[i] = inv[i] - m * row_w
        scale = recips[0]
        for j in range(1, PANEL):
            scale = jnp.where(row == j, recips[j], scale)
        out.append(inv[b] * jnp.sqrt(scale))
        if end < count:
            left = jnp.transpose(rows[b] * scale)[PANEL * end :, :]
            update = nn(left, jnp.concatenate([rows[b], inv[b]], 1), HIGHEST)
            for i in range(end, count):
                part = update[PANEL * (i - end) : PANEL * (i - end + 1), :]
                rows[i] = rows[i] - part[:, :n]
                inv[i] = inv[i] - part[:, n:]
    return jnp.concatenate(out, 0)


def column(row):
    return jnp.transpose(jnp.broadcast_to(row, (RANK, RANK)))


def kernel(
    ny, nx, nz, cols, factor,
    grads, mom_hbm, right_hbm,
    mom_out, right_out, upd_out,
    g_all, g_relay, g_direct, g_mixed, g_summed, mom, right0, buf2,
    p1_part, p1_recv, zbuf, z_part, z_recv,
    m_send, m_recv, m_own, m_slots, m_full, m_other,
    g_part, g_core, g_slots, g_full,
    n_mine, n1_recv, n2_recv, back_own, back_other,
    local_sem, send, recv,
):
    half = cols // 2
    chips = ny * nx
    zr = RANK // nz
    cr = RANK // chips
    y = lax.axis_index("dp")
    r = lax.axis_index("row")
    z = lax.axis_index("col")
    x = r // 2
    c = lax.rem(r, 2)

    def dev(dy=0, dx=0, dc=0, dz=0):
        return {
            "dp": lax.rem(y + dy, ny),
            "row": lax.rem(x + dx, nx) * 2 + lax.rem(c + dc, 2),
            "col": lax.rem(z + dz, nz),
        }

    def hops(d, n):
        return min(d, n - d)

    yz = [(dy, dz) for dz in range(nz) for dy in range(ny) if dy or dz]
    yz.sort(key=lambda d: -hops(d[0], ny) - hops(d[1], nz))
    plane = [(dy, dx) for dy in range(ny) for dx in range(nx) if dy or dx]
    plane.sort(key=lambda d: -hops(d[0], ny) - hops(d[1], nx))
    along_z = sorted(range(1, nz), key=lambda d: -hops(d, nz))
    zc = [(dz, dc) for dz in range(nz) for dc in range(2) if dz or dc]

    met = []
    for dy, dz in yz:
        met.append((dy, 0, 0, dz))
    for dy, dx in plane:
        if (dy, dx, 0, 0) not in met:
            met.append((dy, dx, 0, 0))
    for dz, dc in zc:
        if (0, 0, dc, dz) not in met:
            met.append((0, 0, dc, dz))
    barrier = pltpu.get_barrier_semaphore()
    for offsets in met:
        pl.semaphore_signal(barrier, inc=1, device_id=dev(*offsets), device_id_type=MESH)

    loads = []
    for i, (src, dst) in enumerate([(right_hbm, right0), (grads.at[0], g_all), (mom_hbm, mom)]):
        copy = pltpu.make_async_copy(src, dst, local_sem.at[i])
        copy.start()
        loads.append(copy)
    sent = []

    slots = {}

    def slot_of(name):
        return slots.setdefault(name, len(slots))

    def put(src, dst, name, target):
        slot = slot_of(name)
        pltpu.make_async_remote_copy(
            src_ref=src, dst_ref=dst, send_sem=send.at[slot], recv_sem=recv.at[slot],
            device_id=target, device_id_type=MESH,
        ).start()

    def landed(ref, name):
        slot = slot_of(name)
        copy = pltpu.make_async_remote_copy(
            src_ref=ref, dst_ref=ref, send_sem=send.at[slot], recv_sem=recv.at[slot],
            device_id=dev(), device_id_type=MESH,
        )
        copy.wait_recv()
        sent.append(copy)

    loads[0].wait()
    right_t = jnp.transpose(right0[...])
    loads[1].wait()
    for i in range(ny):
        p1_part[i] = nt(right_t, g_all[pl.ds(i * ROWS_DEV, ROWS_DEV), :])
    loads[2].wait()
    p1_part[y] = p1_part[y] + nt(right_t, mom[...])

    pl.semaphore_wait(barrier, len(met))

    for i, (dy, dz) in enumerate(yz):
        there_y, there_z = lax.rem(y + dy, ny), lax.rem(z + dz, nz)
        put(
            p1_part.at[there_y, pl.ds(pl.multiple_of(there_z * zr, zr), zr), :], p1_recv.at[i],
            "power parts", dev(dy, 0, 0, dz),
        )

    hr = ROWS_DEV // 2
    piece = hr // 2

    def part_rows(owner, start, size):
        return pl.ds(pl.multiple_of(owner * ROWS_DEV + start, size), size)

    after, opposite, before = lax.rem(y + 1, ny), lax.rem(y + 2, ny), lax.rem(y + 3, ny)
    for i in range(2):
        rows = pl.ds(i * piece, piece)
        put(g_all.at[part_rows(opposite, i * piece, piece), :], g_relay.at[0, rows, :], f"relay {i}", dev(1))
        put(g_all.at[part_rows(opposite, hr + i * piece, piece), :], g_relay.at[1, rows, :], f"relay {i}", dev(3))
    put(g_all.at[part_rows(after, hr, hr), :], g_direct.at[1], "direct", dev(1))
    put(g_all.at[part_rows(before, 0, hr), :], g_direct.at[0], "direct", dev(3))

    def forward(i):
        rows = pl.ds(i * piece, piece)
        landed(g_relay.at[:, rows, :], f"relay {i}")
        for side, (owner, start, dy) in enumerate([(after, 0, 1), (before, hr, 3)]):
            own = g_all[part_rows(owner, start + i * piece, piece), :].astype(f32)
            g_mixed[side, rows, :] = (own + g_relay[side, rows, :].astype(f32)).astype(bf16)
            put(g_mixed.at[side, rows, :], g_summed.at[side, rows, :], "summed", dev(dy))

    z_rows = pl.ds(pl.multiple_of(z * zr, zr), zr)

    def gather_z(step, slot):
        for dz in along_z:
            put(zbuf.at[step, z_rows, :], zbuf.at[step, z_rows, :], slot, dev(0, 0, 0, dz))

    forward(0)
    landed(p1_recv, "power parts")
    total = p1_part[y, z_rows, :]
    for i in range(len(yz)):
        total = total + p1_recv[i]
    zbuf[0, z_rows, :] = total
    gather_z(0, "power 1")
    forward(1)
    landed(z_recv, "power 1")

    landed(g_direct, "direct")
    landed(g_summed, "summed")
    for side in range(2):
        rows = pl.ds(side * hr, hr)
        summed = g_all[part_rows(y, side * hr, hr), :].astype(f32)
        summed = summed + g_direct[side].astype(f32) + g_summed[side].astype(f32)
        buffer = (mom[rows, :].astype(f32) + summed).astype(bf16)
        buf2[rows, :] = buffer
        buf2[pl.ds(ROWS_DEV + side * hr, hr), :] = buffer

    mine = pl.ds(pl.multiple_of(c * half, 128), half)
    others = pl.ds(pl.multiple_of((1 - c) * half, 128), half)
    here = y * nx + x
    chip_rows = pl.ds(pl.multiple_of(here * cr, cr), cr)

    cuts = [(0, half)] if half < 512 else [(0, 512), (512, half - 512)]

    def to_plane(name, src, dst):
        for i, (dy, dx) in enumerate(plane):
            there = lax.rem(y + dy, ny) * nx + lax.rem(x + dx, nx)
            rows = pl.ds(pl.multiple_of(there * cr, cr), cr)
            put(src(rows), dst(i), name, dev(dy, dx))

    def reduce_plane(step, power):
        g_part[step] = nt(power, power, HIGHEST)
        put(g_part.at[step], g_core.at[step], f"gram core {step}", dev(0, 0, 1))
        both = jnp.concatenate(halves(power), 1)
        for k, (first, size) in enumerate(cuts):
            where, source = pl.ds(first, size), pl.ds(pl.multiple_of((1 - c) * half + first, 128), size)
            m_send[step, :, where] = nn(both, buf2[:, source])
            put(m_send.at[step, :, where], m_recv.at[step, :, where], f"back core {step}{k}", dev(0, 0, 1))
        for first, size in cuts:
            m_own[step, :, pl.ds(first, size)] = nn(both, buf2[:, pl.ds(pl.multiple_of(c * half + first, 128), size)])
        landed(g_core.at[step], f"gram core {step}")
        g_core[step] = g_part[step] + g_core[step]
        to_plane(f"gram parts {step}", lambda rows: g_core.at[step, rows, :], lambda i: g_slots.at[step, i])
        for k, (first, size) in enumerate(cuts):
            where = pl.ds(first, size)
            landed(m_recv.at[step, :, where], f"back core {step}{k}")
            m_own[step, :, where] = m_own[step, :, where] + m_recv[step, :, where]
            to_plane(
                f"back parts {step}{k}",
                lambda rows: m_own.at[step, rows, where], lambda i: m_slots.at[step, i, :, where],
            )
        landed(g_slots.at[step], f"gram parts {step}")
        total = g_core[step, chip_rows, :]
        for i in range(len(plane)):
            total = total + g_slots[step, i]
        g_full[step, chip_rows, :] = total
        for dy, dx in plane:
            put(g_full.at[step, chip_rows, :], g_full.at[step, chip_rows, :], f"gram {step}", dev(dy, dx))
        for k, (first, size) in enumerate(cuts):
            where = pl.ds(first, size)
            landed(m_slots.at[step, :, :, where], f"back parts {step}{k}")
            total = m_own[step, chip_rows, where]
            for i in range(len(plane)):
                total = total + m_slots[step, i, :, where]
            m_full[step, chip_rows, where] = total
            for dy, dx in plane:
                block = m_full.at[step, chip_rows, where]
                put(block, block, f"back {step}{k}", dev(dy, dx))

    def gram_done(step):
        landed(g_slots.at[step], f"gram {step}")
        return g_full[step]

    def back_done(step, k):
        landed(m_slots.at[step, :, :, pl.ds(*cuts[k])], f"back {step}{k}")

    reduce_plane(0, zbuf[0])
    next_part = jnp.zeros((2 * RANK, ROWS_DEV), f32)
    for k, (first, size) in enumerate(cuts):
        where = pl.ds(first, size)
        back_done(0, k)
        put(m_full.at[0, :, where], m_other.at[:, where], f"back other {k}", dev(0, 0, 1))
        both = jnp.concatenate(halves(m_full[0, :, where]), 0)
        next_part = next_part + nt(both, buf2[0:ROWS_DEV, pl.ds(pl.multiple_of(c * half + first, 128), size)])
    for k, (first, size) in enumerate(cuts):
        where = pl.ds(first, size)
        landed(m_other.at[:, where], f"back other {k}")
        both = jnp.concatenate(halves(m_other[:, where]), 0)
        next_part = next_part + nt(both, buf2[0:ROWS_DEV, pl.ds(pl.multiple_of((1 - c) * half + first, 128), size)])
    z_part[...] = next_part[:RANK] + next_part[RANK:]
    for dz in along_z:
        there = lax.rem(z + dz, nz)
        put(z_part.at[pl.ds(pl.multiple_of(there * zr, zr), zr), :], z_recv.at[dz - 1], "power 2 parts", dev(0, 0, 0, dz))
    w1 = inverse_cholesky(gram_done(0))
    landed(z_recv, "power 2 parts")
    total = z_part[z_rows, :]
    for i in range(nz - 1):
        total = total + z_recv[i]
    zbuf[1, z_rows, :] = total
    gather_z(1, "power 2")
    back_a = nn3(w1, m_full[0])
    back_b = nn3(w1, m_other[...])
    own_sum = jnp.sum(back_a * back_a, axis=1, keepdims=True) + jnp.sum(back_b * back_b, axis=1, keepdims=True)
    own_col = jnp.broadcast_to(own_sum, (RANK, RANK))
    own_row = jnp.transpose(own_col)
    n_mine[0] = own_row[0:8, :]
    for dz in along_z:
        put(n_mine.at[0], n1_recv.at[dz - 1], "norms 1", dev(0, 0, 0, dz))
    landed(z_recv, "power 2")

    power = nn(w1, zbuf[1], HIGHEST) * lax.rsqrt(own_col + 1e-6)
    reduce_plane(1, power)
    landed(n1_recv, "norms 1")
    norm = own_row[0:1, :]
    for i in range(nz - 1):
        norm = norm + n1_recv[i, 0:1, :]
    rest = jnp.sqrt((own_row[0:1, :] + 1e-6) / (norm + 1e-6))
    gram = gram_done(1) * column(rest) * rest
    w2 = inverse_cholesky(gram) * rest
    basis = jnp.transpose(nn(w2, power, HIGHEST)).astype(bf16)
    for k, (first, size) in enumerate(cuts):
        where = pl.ds(first, size)
        back_done(1, k)
        back_own[where, :] = jnp.transpose(nn3(w2, m_full[1, :, where]))
        put(back_own.at[where, :], back_other.at[where, :], "last back", dev(0, 0, 1))
    part = jnp.sum(back_own[...] * back_own[...], axis=0, keepdims=True)
    n_mine[1] = jnp.broadcast_to(part, (8, RANK))
    for i, (dz, dc) in enumerate(zc):
        put(n_mine.at[1], n2_recv.at[i], "norms 2", dev(0, 0, dc, dz))
    mom_out[:, mine] = (
        buf2[0:ROWS_DEV, mine].astype(f32) - 0.25 * nt(basis, back_own[...].astype(bf16))
    ).astype(bf16)
    landed(back_other, "last back")
    mom_out[:, others] = (
        buf2[0:ROWS_DEV, others].astype(f32) - 0.25 * nt(basis, back_other[...].astype(bf16))
    ).astype(bf16)
    landed(n2_recv, "norms 2")
    norm = part
    for i in range(len(zc)):
        norm = norm + n2_recv[i, 0:1, :]
    scale = lax.rsqrt(norm + 1e-6)
    for where, back in ((mine, back_own), (others, back_other)):
        right = (back[...] * scale).astype(bf16)
        right_out[where, :] = right
        upd_out[:, where] = (factor * nt(basis, right)).astype(bf16)
    for copy in sent:
        copy.wait_send()


def solution(mesh):
    ny, nx, nz = mesh.shape["dp"], mesh.shape["row"] // 2, mesh.shape["col"]

    def on_device(grad_parts, momentum, right_prev):
        cols = momentum.shape[1]
        half, chips = cols // 2, ny * nx
        zr, cr = RANK // nz, RANK // chips
        factor = math.sqrt(ny * nx * 2 * ROWS_DEV * cols * nz / RANK)
        vmem = pltpu.VMEM
        any_space = pl.BlockSpec(memory_space=pl.ANY)
        in_vmem = pl.BlockSpec(memory_space=pltpu.VMEM)
        return pl.pallas_call(
            functools.partial(kernel, ny, nx, nz, cols, factor),
            out_shape=(
                jax.ShapeDtypeStruct((ROWS_DEV, cols), bf16),
                jax.ShapeDtypeStruct((cols, RANK), bf16),
                jax.ShapeDtypeStruct((ROWS_DEV, cols), bf16),
            ),
            in_specs=[any_space] * 3,
            out_specs=(in_vmem,) * 3,
            scratch_shapes=[
                vmem((ny * ROWS_DEV, cols), bf16),
                vmem((2, ROWS_DEV // 2, cols), bf16),
                vmem((2, ROWS_DEV // 2, cols), bf16),
                vmem((2, ROWS_DEV // 2, cols), bf16),
                vmem((2, ROWS_DEV // 2, cols), bf16),
                vmem((ROWS_DEV, cols), bf16),
                vmem((cols, RANK), bf16),
                vmem((2 * ROWS_DEV, cols), bf16),
                vmem((ny, RANK, ROWS_DEV), f32),
                vmem((ny * nz - 1, zr, ROWS_DEV), f32),
                vmem((2, RANK, ROWS_DEV), f32),
                vmem((RANK, ROWS_DEV), f32),
                vmem((nz - 1, zr, ROWS_DEV), f32),
                vmem((2, RANK, half), f32),
                vmem((2, RANK, half), f32),
                vmem((2, RANK, half), f32),
                vmem((2, chips - 1, cr, half), f32),
                vmem((2, RANK, half), f32),
                vmem((RANK, half), f32),
                vmem((2, RANK, RANK), f32),
                vmem((2, RANK, RANK), f32),
                vmem((2, chips - 1, cr, RANK), f32),
                vmem((2, RANK, RANK), f32),
                vmem((2, 8, RANK), f32),
                vmem((nz - 1, 8, RANK), f32),
                vmem((2 * nz - 1, 8, RANK), f32),
                vmem((half, RANK), f32),
                vmem((half, RANK), f32),
                pltpu.SemaphoreType.DMA((3,)),
                pltpu.SemaphoreType.DMA((48,)),
                pltpu.SemaphoreType.DMA((48,)),
            ],
            compiler_params=pltpu.CompilerParams(
                collective_id=0, has_side_effects=True, vmem_limit_bytes=63 * 1024 * 1024
            ),
            cost_estimate=pl.CostEstimate(flops=10**9, bytes_accessed=4 * 10**6, transcendentals=0),
        )(grad_parts, momentum, right_prev)

    return jax.shard_map(
        on_device,
        mesh=mesh,
        in_specs=(P("dp", "row", "col"), P(("row", "dp"), "col"), P("col", None)),
        out_specs=(P(("row", "dp"), "col"), P("col", None), P(("row", "dp"), "col")),
        check_vma=False,
    )
```

```python
import functools
import math

import jax
import jax.numpy as jnp
from jax import lax
from jax.experimental import pallas as pl
from jax.experimental.pallas import tpu as pltpu
from jax.sharding import PartitionSpec as P

f32 = jnp.float32
bf16 = jnp.bfloat16
HIGHEST = lax.Precision.HIGHEST
MESH = pl.DeviceIdType.MESH
RANK = 128
ROWS_DEV = 128
PANEL = 8
VMEM_BYTES = 63 * 1024 * 1024
CUTS = [(0, 384), (384, 256), (640, 256)]
EARLY = 2


def nt(a, b, precision=None):
    return lax.dot_general(a, b, (((1,), (1,)), ((), ())), precision=precision, preferred_element_type=f32)


def nn(a, b, precision=None):
    return lax.dot_general(a, b, (((1,), (0,)), ((), ())), precision=precision, preferred_element_type=f32)


def halves(x):
    high = x.astype(bf16)
    return high, (x - high.astype(f32)).astype(bf16)


def nn3(a, b):
    a_high, a_low = halves(a)
    b_high, b_low = halves(b)
    return nn(a_high, b_high) + (nn(a_high, b_low) + nn(a_low, b_high))


def inverse_cholesky(a, ahead=2):
    n, count = RANK, RANK // PANEL
    rows = [a[PANEL * i : PANEL * (i + 1), :] for i in range(count)]
    row = lax.broadcasted_iota(jnp.int32, (PANEL, n), 0)
    lane = lax.broadcasted_iota(jnp.int32, (PANEL, n), 1)
    inv = [(lane == row + PANEL * i).astype(f32) for i in range(count)]
    out = []
    for b in range(count):
        end = min(count, b + 1 + ahead)
        cols = [
            [jnp.broadcast_to(rows[i][:, PANEL * b + k : PANEL * b + k + 1], (PANEL, n)) for k in range(PANEL)]
            for i in range(b, end)
        ]
        recips = []
        for j in range(PANEL):
            recip = 1.0 / jnp.broadcast_to(cols[0][j][j : j + 1, :], (PANEL, n))
            recips.append(recip)
            pivots = [jnp.broadcast_to(cols[0][k][j : j + 1, :], (PANEL, n)) for k in range(j + 1, PANEL)]
            row_a = jnp.broadcast_to(rows[b][j : j + 1, :], (PANEL, n))
            row_w = jnp.broadcast_to(inv[b][j : j + 1, :], (PANEL, n))
            for i in range(b, end):
                m = cols[i - b][j] * recip
                if i == b:
                    m = jnp.where(row > j, m, 0.0)
                for k in range(j + 1, PANEL):
                    cols[i - b][k] = cols[i - b][k] - m * pivots[k - j - 1]
                rows[i] = rows[i] - m * row_a
                inv[i] = inv[i] - m * row_w
        scale = recips[0]
        for j in range(1, PANEL):
            scale = jnp.where(row == j, recips[j], scale)
        out.append(inv[b] * jnp.sqrt(scale))
        if end < count:
            left = jnp.transpose(rows[b] * scale)[PANEL * end :, :]
            update = nn(left, jnp.concatenate([rows[b], inv[b]], 1), HIGHEST)
            for i in range(end, count):
                part = update[PANEL * (i - end) : PANEL * (i - end + 1), :]
                rows[i] = rows[i] - part[:, :n]
                inv[i] = inv[i] - part[:, n:]
    return jnp.concatenate(out, 0)


def column(row):
    return jnp.transpose(jnp.broadcast_to(row, (RANK, RANK)))


def kernel(
    ny, nx, nz, cols,
    grads, mom_hbm, right_hbm,
    mom_out, right_out, basis_out,
    g_all, g_relay, g_direct, g_mixed, g_summed, mom, right0, buf2,
    p1_part, p1_recv, zbuf, z_part, z_recv,
    m_send, m_recv, m_own, m_slots, m_full, m_other,
    g_part, g_core, g_slots, g_full,
    n_mine, n1_recv, n2_recv, back_own, back_other, mom_next, right_next, basis_next,
    local_sem, send, recv,
):
    half = cols // 2
    chips = ny * nx
    zr = RANK // nz
    cr = RANK // chips
    y = lax.axis_index("dp")
    r = lax.axis_index("row")
    z = lax.axis_index("col")
    x = r // 2
    c = lax.rem(r, 2)

    def dev(dy=0, dx=0, dc=0, dz=0):
        return {
            "dp": lax.rem(y + dy, ny),
            "row": lax.rem(x + dx, nx) * 2 + lax.rem(c + dc, 2),
            "col": lax.rem(z + dz, nz),
        }

    def hops(d, n):
        return min(d, n - d)

    yz = [(dy, dz) for dz in range(nz) for dy in range(ny) if dy or dz]
    yz.sort(key=lambda d: -hops(d[0], ny) - hops(d[1], nz))
    plane = [(dy, dx) for dy in range(ny) for dx in range(nx) if dy or dx]
    plane.sort(key=lambda d: -hops(d[0], ny) - hops(d[1], nx))
    along_z = sorted(range(1, nz), key=lambda d: -hops(d, nz))
    zc = [(dz, dc) for dz in range(nz) for dc in range(2) if dz or dc]

    met = []
    for dy, dz in yz:
        met.append((dy, 0, 0, dz))
    for dy, dx in plane:
        if (dy, dx, 0, 0) not in met:
            met.append((dy, dx, 0, 0))
    for dz, dc in zc:
        if (0, 0, dc, dz) not in met:
            met.append((0, 0, dc, dz))
    barrier = pltpu.get_barrier_semaphore()
    for offsets in met:
        pl.semaphore_signal(barrier, inc=1, device_id=dev(*offsets), device_id_type=MESH)

    loads = []
    for i, (src, dst) in enumerate([(right_hbm, right0), (grads.at[0], g_all), (mom_hbm, mom)]):
        copy = pltpu.make_async_copy(src, dst, local_sem.at[i])
        copy.start()
        loads.append(copy)
    sent = []

    slots = {}

    def slot_of(name):
        return slots.setdefault(name, len(slots))

    def put(src, dst, name, target):
        slot = slot_of(name)
        pltpu.make_async_remote_copy(
            src_ref=src, dst_ref=dst, send_sem=send.at[slot], recv_sem=recv.at[slot],
            device_id=target, device_id_type=MESH,
        ).start()

    def landed(ref, name):
        slot = slot_of(name)
        copy = pltpu.make_async_remote_copy(
            src_ref=ref, dst_ref=ref, send_sem=send.at[slot], recv_sem=recv.at[slot],
            device_id=dev(), device_id_type=MESH,
        )
        copy.wait_recv()
        sent.append(copy)

    cuts = CUTS
    hr = ROWS_DEV // 2

    def columns(k):
        first, size = cuts[k]
        return [pl.ds(first, size), pl.ds(half + first, size)]

    def part_rows(owner, start):
        return pl.ds(pl.multiple_of(owner * ROWS_DEV + start, hr), hr)

    after, opposite, before = lax.rem(y + 1, ny), lax.rem(y + 2, ny), lax.rem(y + 3, ny)

    def put_relay(k):
        for where in columns(k):
            put(g_all.at[part_rows(opposite, 0), where], g_relay.at[0, :, where], f"relay {k}", dev(1))
            put(g_all.at[part_rows(opposite, hr), where], g_relay.at[1, :, where], f"relay {k}", dev(3))

    def put_direct(k):
        for where in columns(k):
            put(g_all.at[part_rows(after, hr), where], g_direct.at[1, :, where], f"direct {k}", dev(1))
            put(g_all.at[part_rows(before, 0), where], g_direct.at[0, :, where], f"direct {k}", dev(3))

    def both_columns(ref, k):
        return ref.at[:, :, pl.ds(0, 2 * cuts[k][1])]

    def put_mixed(k):
        landed(both_columns(g_relay, k), f"relay {k}")
        for where in columns(k):
            for side, (owner, start, dy) in enumerate([(after, 0, 1), (before, hr, 3)]):
                own = g_all[part_rows(owner, start), where].astype(f32)
                g_mixed[side, :, where] = (own + g_relay[side, :, where].astype(f32)).astype(bf16)
                put(g_mixed.at[side, :, where], g_summed.at[side, :, where], f"summed {k}", dev(dy))

    def make_buffer(k):
        landed(both_columns(g_direct, k), f"direct {k}")
        landed(both_columns(g_summed, k), f"summed {k}")
        for where in columns(k):
            for side in range(2):
                rows = pl.ds(side * hr, hr)
                total = g_all[part_rows(y, side * hr), where].astype(f32)
                total = total + g_direct[side, :, where].astype(f32) + g_summed[side, :, where].astype(f32)
                buffer = (mom[rows, where].astype(f32) + total).astype(bf16)
                buf2[rows, where] = buffer
                buf2[pl.ds(ROWS_DEV + side * hr, hr), where] = buffer

    loads[0].wait()
    right_t = jnp.transpose(right0[...])
    loads[1].wait()
    for i in range(ny):
        if i == EARLY:
            pl.semaphore_wait(barrier, len(met))
            put_relay(0)
        p1_part[i] = nt(right_t, g_all[pl.ds(i * ROWS_DEV, ROWS_DEV), :])
    loads[2].wait()
    p1_part[y] = p1_part[y] + nt(right_t, mom[...])
    for i, (dy, dz) in enumerate(yz):
        there_y, there_z = lax.rem(y + dy, ny), lax.rem(z + dz, nz)
        put(
            p1_part.at[there_y, pl.ds(pl.multiple_of(there_z * zr, zr), zr), :], p1_recv.at[i],
            "power parts", dev(dy, 0, 0, dz),
        )
    put_direct(0)
    for k in range(1, len(cuts)):
        put_mixed(k - 1)
        put_relay(k)
        put_direct(k)

    z_rows = pl.ds(pl.multiple_of(z * zr, zr), zr)

    def gather_z(step, slot):
        for dz in along_z:
            put(zbuf.at[step, z_rows, :], zbuf.at[step, z_rows, :], slot, dev(0, 0, 0, dz))

    landed(p1_recv, "power parts")
    total = p1_part[y, z_rows, :]
    for i in range(len(yz)):
        total = total + p1_recv[i]
    zbuf[0, z_rows, :] = total
    gather_z(0, "power 1")
    put_mixed(len(cuts) - 1)
    landed(z_recv, "power 1")

    mine = pl.ds(pl.multiple_of(c * half, 128), half)
    others = pl.ds(pl.multiple_of((1 - c) * half, 128), half)
    here = y * nx + x
    chip_rows = pl.ds(pl.multiple_of(here * cr, cr), cr)

    def to_plane(name, src, dst):
        for i, (dy, dx) in enumerate(plane):
            there = lax.rem(y + dy, ny) * nx + lax.rem(x + dx, nx)
            rows = pl.ds(pl.multiple_of(there * cr, cr), cr)
            put(src(rows), dst(i), name, dev(dy, dx))

    def reduce_plane(step, power):
        g_part[step] = nt(power, power, HIGHEST)
        put(g_part.at[step], g_core.at[step], f"gram core {step}", dev(0, 0, 1))
        both = jnp.concatenate(halves(power), 1)

        def to_core(k):
            first, size = cuts[k]
            where, source = pl.ds(first, size), pl.ds(pl.multiple_of((1 - c) * half + first, 128), size)
            m_send[step, :, where] = nn(both, buf2[:, source])
            put(m_send.at[step, :, where], m_recv.at[step, :, where], f"back core {step}{k}", dev(0, 0, 1))
            m_own[step, :, where] = nn(both, buf2[:, pl.ds(pl.multiple_of(c * half + first, 128), size)])

        def parts(k):
            where = pl.ds(*cuts[k])
            landed(m_recv.at[step, :, where], f"back core {step}{k}")
            m_own[step, :, where] = m_own[step, :, where] + m_recv[step, :, where]
            to_plane(
                f"back parts {step}{k}",
                lambda rows: m_own.at[step, rows, where], lambda i: m_slots.at[step, i, :, where],
            )

        def gram_parts():
            landed(g_core.at[step], f"gram core {step}")
            g_core[step] = g_part[step] + g_core[step]
            to_plane(f"gram parts {step}", lambda rows: g_core.at[step, rows, :], lambda i: g_slots.at[step, i])

        if step == 0:
            for k in range(len(cuts)):
                make_buffer(k)
                to_core(k)
                if k == 0:
                    gram_parts()
                parts(k)
        else:
            for k in range(len(cuts)):
                to_core(k)
            gram_parts()
            for k in range(len(cuts)):
                parts(k)
        landed(g_slots.at[step], f"gram parts {step}")
        total = g_core[step, chip_rows, :]
        for i in range(len(plane)):
            total = total + g_slots[step, i]
        g_full[step, chip_rows, :] = total
        for dy, dx in plane:
            put(g_full.at[step, chip_rows, :], g_full.at[step, chip_rows, :], f"gram {step}", dev(dy, dx))
        for k, (first, size) in enumerate(cuts):
            where = pl.ds(first, size)
            landed(m_slots.at[step, :, :, where], f"back parts {step}{k}")
            total = m_own[step, chip_rows, where]
            for i in range(len(plane)):
                total = total + m_slots[step, i, :, where]
            m_full[step, chip_rows, where] = total
            for dy, dx in plane:
                block = m_full.at[step, chip_rows, where]
                put(block, block, f"back {step}{k}", dev(dy, dx))

    def gram_done(step):
        landed(g_slots.at[step], f"gram {step}")
        return g_full[step]

    def back_done(step, k):
        landed(m_slots.at[step, :, :, pl.ds(*cuts[k])], f"back {step}{k}")

    reduce_plane(0, zbuf[0])
    next_part = jnp.zeros((2 * RANK, ROWS_DEV), f32)
    for k, (first, size) in enumerate(cuts):
        where = pl.ds(first, size)
        back_done(0, k)
        put(m_full.at[0, :, where], m_other.at[:, where], f"back other {k}", dev(0, 0, 1))
        both = jnp.concatenate(halves(m_full[0, :, where]), 0)
        next_part = next_part + nt(both, buf2[0:ROWS_DEV, pl.ds(pl.multiple_of(c * half + first, 128), size)])
    for k, (first, size) in enumerate(cuts):
        where = pl.ds(first, size)
        landed(m_other.at[:, where], f"back other {k}")
        both = jnp.concatenate(halves(m_other[:, where]), 0)
        next_part = next_part + nt(both, buf2[0:ROWS_DEV, pl.ds(pl.multiple_of((1 - c) * half + first, 128), size)])
    z_part[...] = next_part[:RANK] + next_part[RANK:]
    for dz in along_z:
        there = lax.rem(z + dz, nz)
        put(z_part.at[pl.ds(pl.multiple_of(there * zr, zr), zr), :], z_recv.at[dz - 1], "power 2 parts", dev(0, 0, 0, dz))
    w1 = inverse_cholesky(gram_done(0))
    landed(z_recv, "power 2 parts")
    total = z_part[z_rows, :]
    for i in range(nz - 1):
        total = total + z_recv[i]
    zbuf[1, z_rows, :] = total
    gather_z(1, "power 2")
    back_a = nn3(w1, m_full[0])
    back_b = nn3(w1, m_other[...])
    own_sum = jnp.sum(back_a * back_a, axis=1, keepdims=True) + jnp.sum(back_b * back_b, axis=1, keepdims=True)
    own_col = jnp.broadcast_to(own_sum, (RANK, RANK))
    own_row = jnp.transpose(own_col)
    n_mine[0] = own_row[0:8, :]
    for dz in along_z:
        put(n_mine.at[0], n1_recv.at[dz - 1], "norms 1", dev(0, 0, 0, dz))
    landed(z_recv, "power 2")

    power = nn(w1, zbuf[1], HIGHEST) * lax.rsqrt(own_col + 1e-6)
    reduce_plane(1, power)
    landed(n1_recv, "norms 1")
    norm = own_row[0:1, :]
    for i in range(nz - 1):
        norm = norm + n1_recv[i, 0:1, :]
    rest = jnp.sqrt((own_row[0:1, :] + 1e-6) / (norm + 1e-6))
    gram = gram_done(1) * column(rest) * rest
    w2 = inverse_cholesky(gram) * rest
    basis = jnp.transpose(nn(w2, power, HIGHEST)).astype(bf16)
    for k, (first, size) in enumerate(cuts):
        where = pl.ds(first, size)
        back_done(1, k)
        back_own[where, :] = jnp.transpose(nn3(w2, m_full[1, :, where]))
        put(back_own.at[where, :], back_other.at[where, :], "last back", dev(0, 0, 1))
    part = jnp.sum(back_own[...] * back_own[...], axis=0, keepdims=True)
    n_mine[1] = jnp.broadcast_to(part, (8, RANK))
    for i, (dz, dc) in enumerate(zc):
        put(n_mine.at[1], n2_recv.at[i], "norms 2", dev(0, 0, dc, dz))
    mom_next[:, mine] = (
        buf2[0:ROWS_DEV, mine].astype(f32) - 0.25 * nt(basis, back_own[...].astype(bf16))
    ).astype(bf16)
    basis_next[...] = basis
    landed(back_other, "last back")
    mom_next[:, others] = (
        buf2[0:ROWS_DEV, others].astype(f32) - 0.25 * nt(basis, back_other[...].astype(bf16))
    ).astype(bf16)
    stores = [
        pltpu.make_async_copy(mom_next, mom_out, local_sem.at[3]),
        pltpu.make_async_copy(basis_next, basis_out, local_sem.at[4]),
        pltpu.make_async_copy(right_next, right_out, local_sem.at[5]),
    ]
    stores[0].start()
    stores[1].start()
    landed(n2_recv, "norms 2")
    norm = part
    for i in range(len(zc)):
        norm = norm + n2_recv[i, 0:1, :]
    scale = lax.rsqrt(norm + 1e-6)
    right_next[mine, :] = (back_own[...] * scale).astype(bf16)
    right_next[others, :] = (back_other[...] * scale).astype(bf16)
    stores[2].start()
    for copy in sent:
        copy.wait_send()
    for copy in stores:
        copy.wait()


def finish(factor, mom_in, right_in, basis_in, mom_out, right_out, upd_out, mom, right, basis, upd, sem):
    loads = [
        pltpu.make_async_copy(src, dst, sem.at[i])
        for i, (src, dst) in enumerate([(basis_in, basis), (right_in, right), (mom_in, mom)])
    ]
    for copy in loads:
        copy.start()
    stores = [pltpu.make_async_copy(right, right_out, sem.at[3]), pltpu.make_async_copy(mom, mom_out, sem.at[4])]
    loads[0].wait()
    loads[1].wait()
    stores[0].start()
    half = upd.shape[1] // 2
    for i in range(2):
        where = pl.ds(i * half, half)
        upd[:, where] = (factor * nt(basis[...], right[where, :])).astype(bf16)
        if i == 0:
            loads[2].wait()
            stores[1].start()
        stores.append(pltpu.make_async_copy(upd.at[:, where], upd_out.at[:, where], sem.at[5 + i]))
        stores[-1].start()
    for copy in stores:
        copy.wait()


def solution(mesh):
    ny, nx, nz = mesh.shape["dp"], mesh.shape["row"] // 2, mesh.shape["col"]

    def on_device(grad_parts, momentum, right_prev):
        cols = momentum.shape[1]
        half, chips = cols // 2, ny * nx
        zr, cr = RANK // nz, RANK // chips
        factor = math.sqrt(ny * nx * 2 * ROWS_DEV * cols * nz / RANK)
        vmem = pltpu.VMEM
        any_space = pl.BlockSpec(memory_space=pl.ANY)
        mom_shape = jax.ShapeDtypeStruct((ROWS_DEV, cols), bf16)
        right_shape = jax.ShapeDtypeStruct((cols, RANK), bf16)
        results = pl.pallas_call(
            functools.partial(kernel, ny, nx, nz, cols),
            out_shape=(mom_shape, right_shape, jax.ShapeDtypeStruct((ROWS_DEV, RANK), bf16)),
            in_specs=[any_space] * 3,
            out_specs=(any_space,) * 3,
            scratch_shapes=[
                vmem((ny * ROWS_DEV, cols), bf16),
                vmem((2, ROWS_DEV // 2, cols), bf16),
                vmem((2, ROWS_DEV // 2, cols), bf16),
                vmem((2, ROWS_DEV // 2, cols), bf16),
                vmem((2, ROWS_DEV // 2, cols), bf16),
                vmem((ROWS_DEV, cols), bf16),
                vmem((cols, RANK), bf16),
                vmem((2 * ROWS_DEV, cols), bf16),
                vmem((ny, RANK, ROWS_DEV), f32),
                vmem((ny * nz - 1, zr, ROWS_DEV), f32),
                vmem((2, RANK, ROWS_DEV), f32),
                vmem((RANK, ROWS_DEV), f32),
                vmem((nz - 1, zr, ROWS_DEV), f32),
                vmem((2, RANK, half), f32),
                vmem((2, RANK, half), f32),
                vmem((2, RANK, half), f32),
                vmem((2, chips - 1, cr, half), f32),
                vmem((2, RANK, half), f32),
                vmem((RANK, half), f32),
                vmem((2, RANK, RANK), f32),
                vmem((2, RANK, RANK), f32),
                vmem((2, chips - 1, cr, RANK), f32),
                vmem((2, RANK, RANK), f32),
                vmem((2, 8, RANK), f32),
                vmem((nz - 1, 8, RANK), f32),
                vmem((2 * nz - 1, 8, RANK), f32),
                vmem((half, RANK), f32),
                vmem((half, RANK), f32),
                vmem((ROWS_DEV, cols), bf16),
                vmem((cols, RANK), bf16),
                vmem((ROWS_DEV, RANK), bf16),
                pltpu.SemaphoreType.DMA((6,)),
                pltpu.SemaphoreType.DMA((48,)),
                pltpu.SemaphoreType.DMA((48,)),
            ],
            compiler_params=pltpu.CompilerParams(
                collective_id=0, has_side_effects=True, vmem_limit_bytes=VMEM_BYTES
            ),
            cost_estimate=pl.CostEstimate(flops=10**9, bytes_accessed=4 * 10**6, transcendentals=0),
        )(grad_parts, momentum, right_prev)
        return pl.pallas_call(
            functools.partial(finish, factor),
            out_shape=(mom_shape, right_shape, mom_shape),
            in_specs=[any_space] * 3,
            out_specs=(any_space,) * 3,
            scratch_shapes=[
                vmem((ROWS_DEV, cols), bf16),
                vmem((cols, RANK), bf16),
                vmem((ROWS_DEV, RANK), bf16),
                vmem((ROWS_DEV, cols), bf16),
                pltpu.SemaphoreType.DMA((7,)),
            ],
            compiler_params=pltpu.CompilerParams(vmem_limit_bytes=VMEM_BYTES),
            cost_estimate=pl.CostEstimate(flops=6 * 10**7, bytes_accessed=3 * 10**6, transcendentals=0),
        )(*results)

    return jax.shard_map(
        on_device,
        mesh=mesh,
        in_specs=(P("dp", "row", "col"), P(("row", "dp"), "col"), P("col", None)),
        out_specs=(P(("row", "dp"), "col"), P("col", None), P(("row", "dp"), "col")),
        check_vma=False,
    )
```

```python
import functools
import math

import jax
import jax.numpy as jnp
from jax import lax
from jax.experimental import pallas as pl
from jax.experimental.pallas import tpu as pltpu
from jax.sharding import PartitionSpec as P

f32 = jnp.float32
bf16 = jnp.bfloat16
HIGHEST = lax.Precision.HIGHEST
MESH = pl.DeviceIdType.MESH
RANK = 128
ROWS_DEV = 128
PANEL = 8
VMEM_BYTES = 63 * 1024 * 1024
CUTS = [(0, 384), (384, 256), (640, 256)]
LAST = [(0, 384), (384, 256), (640, 256)]
EARLY = 2


def nt(a, b, precision=None):
    return lax.dot_general(a, b, (((1,), (1,)), ((), ())), precision=precision, preferred_element_type=f32)


def nn(a, b, precision=None):
    return lax.dot_general(a, b, (((1,), (0,)), ((), ())), precision=precision, preferred_element_type=f32)


def halves(x):
    high = x.astype(bf16)
    return high, (x - high.astype(f32)).astype(bf16)


def nn3(a, b):
    a_high, a_low = halves(a)
    b_high, b_low = halves(b)
    return nn(a_high, b_high) + (nn(a_high, b_low) + nn(a_low, b_high))


def inverse_cholesky(a, ahead=2):
    n, count = RANK, RANK // PANEL
    rows = [a[PANEL * i : PANEL * (i + 1), :] for i in range(count)]
    row = lax.broadcasted_iota(jnp.int32, (PANEL, n), 0)
    lane = lax.broadcasted_iota(jnp.int32, (PANEL, n), 1)
    inv = [(lane == row + PANEL * i).astype(f32) for i in range(count)]
    out = []
    for b in range(count):
        end = min(count, b + 1 + ahead)
        cols = [
            [jnp.broadcast_to(rows[i][:, PANEL * b + k : PANEL * b + k + 1], (PANEL, n)) for k in range(PANEL)]
            for i in range(b, end)
        ]
        recips = []
        for j in range(PANEL):
            recip = 1.0 / jnp.broadcast_to(cols[0][j][j : j + 1, :], (PANEL, n))
            recips.append(recip)
            pivots = [jnp.broadcast_to(cols[0][k][j : j + 1, :], (PANEL, n)) for k in range(j + 1, PANEL)]
            row_a = jnp.broadcast_to(rows[b][j : j + 1, :], (PANEL, n))
            row_w = jnp.broadcast_to(inv[b][j : j + 1, :], (PANEL, n))
            for i in range(b, end):
                m = cols[i - b][j] * recip
                if i == b:
                    m = jnp.where(row > j, m, 0.0)
                for k in range(j + 1, PANEL):
                    cols[i - b][k] = cols[i - b][k] - m * pivots[k - j - 1]
                rows[i] = rows[i] - m * row_a
                inv[i] = inv[i] - m * row_w
        scale = recips[0]
        for j in range(1, PANEL):
            scale = jnp.where(row == j, recips[j], scale)
        out.append(inv[b] * jnp.sqrt(scale))
        if end < count:
            left = jnp.transpose(rows[b] * scale)[PANEL * end :, :]
            update = nn(left, jnp.concatenate([rows[b], inv[b]], 1), HIGHEST)
            for i in range(end, count):
                part = update[PANEL * (i - end) : PANEL * (i - end + 1), :]
                rows[i] = rows[i] - part[:, :n]
                inv[i] = inv[i] - part[:, n:]
    return jnp.concatenate(out, 0)


def column(row):
    return jnp.transpose(jnp.broadcast_to(row, (RANK, RANK)))


def kernel(
    ny, nx, nz, cols,
    grads, mom_hbm, right_hbm,
    mom_out, right_out, basis_out,
    g_all, g_relay, g_direct, g_mixed, g_summed, mom, right0, buf2,
    p1_part, p1_recv, zbuf, z_part, z_recv,
    chip_buf, chip_power, m_own, m_slots, m_full, m_other,
    g_core, g_slots, g_full,
    n_mine, n1_recv, n2_recv, back_own, back_other, mom_next, right_next, basis_next,
    local_sem, send, recv,
):
    half = cols // 2
    chips = ny * nx
    zr = RANK // nz
    cr = RANK // chips
    y = lax.axis_index("dp")
    r = lax.axis_index("row")
    z = lax.axis_index("col")
    x = r // 2
    c = lax.rem(r, 2)

    def dev(dy=0, dx=0, dc=0, dz=0):
        return {
            "dp": lax.rem(y + dy, ny),
            "row": lax.rem(x + dx, nx) * 2 + lax.rem(c + dc, 2),
            "col": lax.rem(z + dz, nz),
        }

    def hops(d, n):
        return min(d, n - d)

    yz = [(dy, dz) for dz in range(nz) for dy in range(ny) if dy or dz]
    yz.sort(key=lambda d: -hops(d[0], ny) - hops(d[1], nz))
    plane = [(dy, dx) for dy in range(ny) for dx in range(nx) if dy or dx]
    plane.sort(key=lambda d: -hops(d[0], ny) - hops(d[1], nx))
    along_z = sorted(range(1, nz), key=lambda d: -hops(d, nz))
    zc = [(dz, dc) for dz in range(nz) for dc in range(2) if dz or dc]

    met = []
    for dy, dz in yz:
        met.append((dy, 0, 0, dz))
    for dy, dx in plane:
        if (dy, dx, 0, 0) not in met:
            met.append((dy, dx, 0, 0))
    for dz, dc in zc:
        if (0, 0, dc, dz) not in met:
            met.append((0, 0, dc, dz))
    loads = []
    for i, (src, dst) in enumerate([(right_hbm, right0), (grads.at[0], g_all), (mom_hbm, mom)]):
        copy = pltpu.make_async_copy(src, dst, local_sem.at[i])
        copy.start()
        loads.append(copy)
    barrier = pltpu.get_barrier_semaphore()
    for offsets in met:
        pl.semaphore_signal(barrier, inc=1, device_id=dev(*offsets), device_id_type=MESH)

    sent = []

    slots = {}

    def slot_of(name):
        return slots.setdefault(name, len(slots))

    def put(src, dst, name, target):
        slot = slot_of(name)
        pltpu.make_async_remote_copy(
            src_ref=src, dst_ref=dst, send_sem=send.at[slot], recv_sem=recv.at[slot],
            device_id=target, device_id_type=MESH,
        ).start()

    def landed(ref, name):
        slot = slot_of(name)
        copy = pltpu.make_async_remote_copy(
            src_ref=ref, dst_ref=ref, send_sem=send.at[slot], recv_sem=recv.at[slot],
            device_id=dev(), device_id_type=MESH,
        )
        copy.wait_recv()
        sent.append(copy)

    cuts = CUTS
    last = LAST
    hr = ROWS_DEV // 2

    def columns(k):
        first, size = cuts[k]
        return [pl.ds(first, size), pl.ds(half + first, size)]

    def part_rows(owner, start):
        return pl.ds(pl.multiple_of(owner * ROWS_DEV + start, hr), hr)

    after, opposite, before = lax.rem(y + 1, ny), lax.rem(y + 2, ny), lax.rem(y + 3, ny)

    def put_relay(k):
        for where in columns(k):
            put(g_all.at[part_rows(opposite, 0), where], g_relay.at[0, :, where], f"relay {k}", dev(1))
            put(g_all.at[part_rows(opposite, hr), where], g_relay.at[1, :, where], f"relay {k}", dev(3))

    def put_direct(k):
        for where in columns(k):
            put(g_all.at[part_rows(after, hr), where], g_direct.at[1, :, where], f"direct {k}", dev(1))
            put(g_all.at[part_rows(before, 0), where], g_direct.at[0, :, where], f"direct {k}", dev(3))

    def both_columns(ref, k):
        return ref.at[:, :, pl.ds(0, 2 * cuts[k][1])]

    def put_mixed(k):
        landed(both_columns(g_relay, k), f"relay {k}")
        for where in columns(k):
            for side, (owner, start, dy) in enumerate([(after, 0, 1), (before, hr, 3)]):
                own = g_all[part_rows(owner, start), where].astype(f32)
                g_mixed[side, :, where] = (own + g_relay[side, :, where].astype(f32)).astype(bf16)
                put(g_mixed.at[side, :, where], g_summed.at[side, :, where], f"summed {k}", dev(dy))

    def make_buffer(k):
        landed(both_columns(g_direct, k), f"direct {k}")
        landed(both_columns(g_summed, k), f"summed {k}")
        for where in columns(k):
            for side in range(2):
                rows = pl.ds(side * hr, hr)
                total = g_all[part_rows(y, side * hr), where].astype(f32)
                total = total + g_direct[side, :, where].astype(f32) + g_summed[side, :, where].astype(f32)
                buffer = (mom[rows, where].astype(f32) + total).astype(bf16)
                buf2[rows, where] = buffer
        first, size = cuts[k]
        ours = pl.ds(pl.multiple_of(c * half + first, 128), size)
        theirs = pl.ds(pl.multiple_of((1 - c) * half + first, 128), size)
        chip_buf[c, :, pl.ds(first, size)] = buf2[:, ours]
        put(buf2.at[:, theirs], chip_buf.at[c, :, pl.ds(first, size)], f"buffer {k}", dev(0, 0, 1))

    loads[0].wait()
    right_t = jnp.transpose(right0[...])
    loads[1].wait()
    for i in range(ny):
        if i == EARLY:
            pl.semaphore_wait(barrier, len(met))
            put_relay(0)
        p1_part[i] = nt(right_t, g_all[pl.ds(i * ROWS_DEV, ROWS_DEV), :])
    loads[2].wait()
    p1_part[y] = p1_part[y] + nt(right_t, mom[...])
    for i, (dy, dz) in enumerate(yz):
        there_y, there_z = lax.rem(y + dy, ny), lax.rem(z + dz, nz)
        put(
            p1_part.at[there_y, pl.ds(pl.multiple_of(there_z * zr, zr), zr), :], p1_recv.at[i],
            "power parts", dev(dy, 0, 0, dz),
        )
    put_relay(1)
    put_direct(0)
    put_relay(2)
    put_direct(1)
    put_mixed(0)
    put_direct(2)
    put_mixed(1)
    z_rows = pl.ds(pl.multiple_of(z * zr, zr), zr)

    def gather_z(step, slot):
        for dz in along_z:
            put(zbuf.at[step, z_rows, :], zbuf.at[step, z_rows, :], slot, dev(0, 0, 0, dz))

    landed(p1_recv, "power parts")
    total = p1_part[y, z_rows, :]
    for i in range(len(yz)):
        total = total + p1_recv[i]
    zbuf[0, z_rows, :] = total
    gather_z(0, "power 1")
    put_mixed(2)
    landed(z_recv, "power 1")

    mine = pl.ds(pl.multiple_of(c * half, 128), half)
    others = pl.ds(pl.multiple_of((1 - c) * half, 128), half)
    here = y * nx + x
    chip_rows = pl.ds(pl.multiple_of(here * cr, cr), cr)

    def to_plane(name, src, dst):
        for i, (dy, dx) in enumerate(plane):
            there = lax.rem(y + dy, ny) * nx + lax.rem(x + dx, nx)
            rows = pl.ds(pl.multiple_of(there * cr, cr), cr)
            put(src(rows), dst(i), name, dev(dy, dx))

    def reduce_plane(step, power):
        cuts = CUTS if step == 0 else LAST
        chip_power[step, c] = power
        put(chip_power.at[step, c], chip_power.at[step, c], f"power core {step}", dev(0, 0, 1))
        landed(chip_power.at[step, 0], f"power core {step}")
        power = jnp.concatenate([chip_power[step, 0], chip_power[step, 1]], 1)
        high, low = halves(power)

        def product(k):
            where = pl.ds(*cuts[k])
            rows = jnp.concatenate([chip_buf[0, :, where], chip_buf[1, :, where]], 0)
            m_own[step, :, where] = nn(high, rows) + nn(low, rows)

        def parts(k):
            where = pl.ds(*cuts[k])
            to_plane(
                f"back parts {step}{k}",
                lambda rows: m_own.at[step, rows, where], lambda i: m_slots.at[step, i, :, where],
            )

        def gram_parts():
            g_core[step] = nt(power, power, HIGHEST)
            to_plane(f"gram parts {step}", lambda rows: g_core.at[step, rows, :], lambda i: g_slots.at[step, i])

        for k in range(len(cuts)):
            if step == 0:
                make_buffer(k)
                if k == 0:
                    gram_parts()
                landed(chip_buf.at[0, :, pl.ds(*cuts[k])], f"buffer {k}")
            if step == 1 and k == 0:
                gram_parts()
            product(k)
            parts(k)
        landed(g_slots.at[step], f"gram parts {step}")
        total = g_core[step, chip_rows, :]
        for i in range(len(plane)):
            total = total + g_slots[step, i]
        g_full[step, chip_rows, :] = total
        for dy, dx in plane:
            put(g_full.at[step, chip_rows, :], g_full.at[step, chip_rows, :], f"gram {step}", dev(dy, dx))
        for k, (first, size) in enumerate(cuts):
            where = pl.ds(first, size)
            landed(m_slots.at[step, :, :, where], f"back parts {step}{k}")
            total = m_own[step, chip_rows, where]
            for i in range(len(plane)):
                total = total + m_slots[step, i, :, where]
            m_full[step, chip_rows, where] = total
            for dy, dx in plane:
                block = m_full.at[step, chip_rows, where]
                put(block, block, f"back {step}{k}", dev(dy, dx))

    def gram_done(step):
        landed(g_slots.at[step], f"gram {step}")
        return g_full[step]

    def back_done(step, k):
        landed(m_slots.at[step, :, :, pl.ds(*(cuts, last)[step][k])], f"back {step}{k}")

    reduce_plane(0, zbuf[0])
    next_part = jnp.zeros((2 * RANK, ROWS_DEV), f32)
    for k, (first, size) in enumerate(cuts):
        where = pl.ds(first, size)
        back_done(0, k)
        put(m_full.at[0, :, where], m_other.at[:, where], f"back other {k}", dev(0, 0, 1))
        both = jnp.concatenate(halves(m_full[0, :, where]), 0)
        next_part = next_part + nt(both, buf2[:, pl.ds(pl.multiple_of(c * half + first, 128), size)])
    for k, (first, size) in enumerate(cuts):
        where = pl.ds(first, size)
        landed(m_other.at[:, where], f"back other {k}")
        both = jnp.concatenate(halves(m_other[:, where]), 0)
        next_part = next_part + nt(both, buf2[:, pl.ds(pl.multiple_of((1 - c) * half + first, 128), size)])
    z_part[...] = next_part[:RANK] + next_part[RANK:]
    for dz in along_z:
        there = lax.rem(z + dz, nz)
        put(z_part.at[pl.ds(pl.multiple_of(there * zr, zr), zr), :], z_recv.at[dz - 1], "power 2 parts", dev(0, 0, 0, dz))
    w1 = inverse_cholesky(gram_done(0))
    landed(z_recv, "power 2 parts")
    total = z_part[z_rows, :]
    for i in range(nz - 1):
        total = total + z_recv[i]
    zbuf[1, z_rows, :] = total
    gather_z(1, "power 2")
    back_a = nn3(w1, m_full[0])
    back_b = nn3(w1, m_other[...])
    own_sum = jnp.sum(back_a * back_a, axis=1, keepdims=True) + jnp.sum(back_b * back_b, axis=1, keepdims=True)
    own_col = jnp.broadcast_to(own_sum, (RANK, RANK))
    own_row = jnp.transpose(own_col)
    n_mine[0] = own_row[0:8, :]
    for dz in along_z:
        put(n_mine.at[0], n1_recv.at[dz - 1], "norms 1", dev(0, 0, 0, dz))
    landed(z_recv, "power 2")

    power = nn(w1, zbuf[1], HIGHEST) * lax.rsqrt(own_col + 1e-6)
    reduce_plane(1, power)
    landed(n1_recv, "norms 1")
    norm = own_row[0:1, :]
    for i in range(nz - 1):
        norm = norm + n1_recv[i, 0:1, :]
    rest = jnp.sqrt((own_row[0:1, :] + 1e-6) / (norm + 1e-6))
    gram = gram_done(1) * column(rest) * rest
    w2 = inverse_cholesky(gram) * rest
    basis = jnp.transpose(nn(w2, power, HIGHEST)).astype(bf16)
    for k, (first, size) in enumerate(last):
        where = pl.ds(first, size)
        back_done(1, k)
        back_own[where, :] = jnp.transpose(nn3(w2, m_full[1, :, where]))
        put(back_own.at[where, :], back_other.at[where, :], "last back", dev(0, 0, 1))
    part = jnp.sum(back_own[...] * back_own[...], axis=0, keepdims=True)
    n_mine[1] = jnp.broadcast_to(part, (8, RANK))
    for i, (dz, dc) in enumerate(zc):
        put(n_mine.at[1], n2_recv.at[i], "norms 2", dev(0, 0, dc, dz))
    mom_next[:, mine] = (
        buf2[:, mine].astype(f32) - 0.25 * nt(basis, back_own[...].astype(bf16))
    ).astype(bf16)
    basis_next[...] = basis
    landed(back_other, "last back")
    mom_next[:, others] = (
        buf2[:, others].astype(f32) - 0.25 * nt(basis, back_other[...].astype(bf16))
    ).astype(bf16)
    stores = [
        pltpu.make_async_copy(mom_next, mom_out, local_sem.at[3]),
        pltpu.make_async_copy(basis_next, basis_out, local_sem.at[4]),
        pltpu.make_async_copy(right_next, right_out, local_sem.at[5]),
    ]
    stores[0].start()
    stores[1].start()
    landed(n2_recv, "norms 2")
    norm = part
    for i in range(len(zc)):
        norm = norm + n2_recv[i, 0:1, :]
    scale = lax.rsqrt(norm + 1e-6)
    right_next[mine, :] = (back_own[...] * scale).astype(bf16)
    right_next[others, :] = (back_other[...] * scale).astype(bf16)
    stores[2].start()
    for copy in sent:
        copy.wait_send()
    for copy in stores:
        copy.wait()


def finish(factor, mom_in, right_in, basis_in, mom_out, right_out, upd_out, mom, right, basis, upd, sem):
    loads = [
        pltpu.make_async_copy(src, dst, sem.at[i])
        for i, (src, dst) in enumerate([(basis_in, basis), (right_in, right), (mom_in, mom)])
    ]
    for copy in loads:
        copy.start()
    stores = [pltpu.make_async_copy(right, right_out, sem.at[3]), pltpu.make_async_copy(mom, mom_out, sem.at[4])]
    loads[0].wait()
    loads[1].wait()
    stores[0].start()
    half = upd.shape[1] // 2
    for i in range(2):
        where = pl.ds(i * half, half)
        upd[:, where] = (factor * nt(basis[...], right[where, :])).astype(bf16)
        if i == 0:
            loads[2].wait()
            stores[1].start()
        stores.append(pltpu.make_async_copy(upd.at[:, where], upd_out.at[:, where], sem.at[5 + i]))
        stores[-1].start()
    for copy in stores:
        copy.wait()


def solution(mesh):
    ny, nx, nz = mesh.shape["dp"], mesh.shape["row"] // 2, mesh.shape["col"]

    def on_device(grad_parts, momentum, right_prev):
        cols = momentum.shape[1]
        half, chips = cols // 2, ny * nx
        zr, cr = RANK // nz, RANK // chips
        factor = math.sqrt(ny * nx * 2 * ROWS_DEV * cols * nz / RANK)
        vmem = pltpu.VMEM
        any_space = pl.BlockSpec(memory_space=pl.ANY)
        mom_shape = jax.ShapeDtypeStruct((ROWS_DEV, cols), bf16)
        right_shape = jax.ShapeDtypeStruct((cols, RANK), bf16)
        results = pl.pallas_call(
            functools.partial(kernel, ny, nx, nz, cols),
            out_shape=(mom_shape, right_shape, jax.ShapeDtypeStruct((ROWS_DEV, RANK), bf16)),
            in_specs=[any_space] * 3,
            out_specs=(any_space,) * 3,
            scratch_shapes=[
                vmem((ny * ROWS_DEV, cols), bf16),
                vmem((2, ROWS_DEV // 2, cols), bf16),
                vmem((2, ROWS_DEV // 2, cols), bf16),
                vmem((2, ROWS_DEV // 2, cols), bf16),
                vmem((2, ROWS_DEV // 2, cols), bf16),
                vmem((ROWS_DEV, cols), bf16),
                vmem((cols, RANK), bf16),
                vmem((ROWS_DEV, cols), bf16),
                vmem((ny, RANK, ROWS_DEV), f32),
                vmem((ny * nz - 1, zr, ROWS_DEV), f32),
                vmem((2, RANK, ROWS_DEV), f32),
                vmem((RANK, ROWS_DEV), f32),
                vmem((nz - 1, zr, ROWS_DEV), f32),
                vmem((2, ROWS_DEV, half), bf16),
                vmem((2, 2, RANK, ROWS_DEV), f32),
                vmem((2, RANK, half), f32),
                vmem((2, chips - 1, cr, half), f32),
                vmem((2, RANK, half), f32),
                vmem((RANK, half), f32),
                vmem((2, RANK, RANK), f32),
                vmem((2, chips - 1, cr, RANK), f32),
                vmem((2, RANK, RANK), f32),
                vmem((2, 8, RANK), f32),
                vmem((nz - 1, 8, RANK), f32),
                vmem((2 * nz - 1, 8, RANK), f32),
                vmem((half, RANK), f32),
                vmem((half, RANK), f32),
                vmem((ROWS_DEV, cols), bf16),
                vmem((cols, RANK), bf16),
                vmem((ROWS_DEV, RANK), bf16),
                pltpu.SemaphoreType.DMA((6,)),
                pltpu.SemaphoreType.DMA((48,)),
                pltpu.SemaphoreType.DMA((48,)),
            ],
            compiler_params=pltpu.CompilerParams(
                collective_id=0, has_side_effects=True, vmem_limit_bytes=VMEM_BYTES
            ),
            cost_estimate=pl.CostEstimate(flops=10**9, bytes_accessed=4 * 10**6, transcendentals=0),
        )(grad_parts, momentum, right_prev)
        return pl.pallas_call(
            functools.partial(finish, factor),
            out_shape=(mom_shape, right_shape, mom_shape),
            in_specs=[any_space] * 3,
            out_specs=(any_space,) * 3,
            scratch_shapes=[
                vmem((ROWS_DEV, cols), bf16),
                vmem((cols, RANK), bf16),
                vmem((ROWS_DEV, RANK), bf16),
                vmem((ROWS_DEV, cols), bf16),
                pltpu.SemaphoreType.DMA((7,)),
            ],
            compiler_params=pltpu.CompilerParams(vmem_limit_bytes=VMEM_BYTES),
            cost_estimate=pl.CostEstimate(flops=6 * 10**7, bytes_accessed=3 * 10**6, transcendentals=0),
        )(*results)

    return jax.shard_map(
        on_device,
        mesh=mesh,
        in_specs=(P("dp", "row", "col"), P(("row", "dp"), "col"), P("col", None)),
        out_specs=(P(("row", "dp"), "col"), P("col", None), P(("row", "dp"), "col")),
        check_vma=False,
    )
```

```python
import functools
import math

import jax
import jax.numpy as jnp
from jax import lax
from jax.experimental import pallas as pl
from jax.experimental.pallas import tpu as pltpu
from jax.sharding import PartitionSpec as P

f32 = jnp.float32
bf16 = jnp.bfloat16
HIGHEST = lax.Precision.HIGHEST
MESH = pl.DeviceIdType.MESH
RANK = 128
ROWS_DEV = 128
PANEL = 8
VMEM_BYTES = 63 * 1024 * 1024
CUTS = [(0, 384), (384, 256), (640, 256)]
LAST = [(0, 384), (384, 256), (640, 256)]
EARLY = 2


def nt(a, b, precision=None):
    return lax.dot_general(a, b, (((1,), (1,)), ((), ())), precision=precision, preferred_element_type=f32)


def nn(a, b, precision=None):
    return lax.dot_general(a, b, (((1,), (0,)), ((), ())), precision=precision, preferred_element_type=f32)


def halves(x):
    high = x.astype(bf16)
    return high, (x - high.astype(f32)).astype(bf16)


def nn3(a, b):
    a_high, a_low = halves(a)
    b_high, b_low = halves(b)
    return nn(a_high, b_high) + (nn(a_high, b_low) + nn(a_low, b_high))


def inverse_cholesky(a, ahead=2):
    n, count = RANK, RANK // PANEL
    rows = [a[PANEL * i : PANEL * (i + 1), :] for i in range(count)]
    row = lax.broadcasted_iota(jnp.int32, (PANEL, n), 0)
    lane = lax.broadcasted_iota(jnp.int32, (PANEL, n), 1)
    inv = [(lane == row + PANEL * i).astype(f32) for i in range(count)]
    out = []
    for b in range(count):
        end = min(count, b + 1 + ahead)
        cols = [
            [jnp.broadcast_to(rows[i][:, PANEL * b + k : PANEL * b + k + 1], (PANEL, n)) for k in range(PANEL)]
            for i in range(b, end)
        ]
        recips = []
        for j in range(PANEL):
            recip = 1.0 / jnp.broadcast_to(cols[0][j][j : j + 1, :], (PANEL, n))
            recips.append(recip)
            pivots = [jnp.broadcast_to(cols[0][k][j : j + 1, :], (PANEL, n)) for k in range(j + 1, PANEL)]
            row_a = jnp.broadcast_to(rows[b][j : j + 1, :], (PANEL, n))
            row_w = jnp.broadcast_to(inv[b][j : j + 1, :], (PANEL, n))
            for i in range(b, end):
                m = cols[i - b][j] * recip
                if i == b:
                    m = jnp.where(row > j, m, 0.0)
                for k in range(j + 1, PANEL):
                    cols[i - b][k] = cols[i - b][k] - m * pivots[k - j - 1]
                rows[i] = rows[i] - m * row_a
                inv[i] = inv[i] - m * row_w
        scale = recips[0]
        for j in range(1, PANEL):
            scale = jnp.where(row == j, recips[j], scale)
        out.append(inv[b] * jnp.sqrt(scale))
        if end < count:
            left = jnp.transpose(rows[b] * scale)[PANEL * end :, :]
            update = nn(left, jnp.concatenate([rows[b], inv[b]], 1), HIGHEST)
            for i in range(end, count):
                part = update[PANEL * (i - end) : PANEL * (i - end + 1), :]
                rows[i] = rows[i] - part[:, :n]
                inv[i] = inv[i] - part[:, n:]
    return jnp.concatenate(out, 0)


def column(row):
    return jnp.transpose(jnp.broadcast_to(row, (RANK, RANK)))


def kernel(
    ny, nx, nz, cols,
    grads, mom_hbm, right_hbm,
    mom_out, right_out, basis_out,
    g_all, g_relay, g_direct, g_mixed, g_summed, mom, right0, buf2,
    p1_part, p1_recv, zbuf, z_part, z_recv,
    chip_buf, chip_power, m_own, m_slots, m_full, m_other,
    g_core, g_slots, g_full,
    n_mine, n1_recv, n2_recv, back_own, back_other, mom_next, right_next, basis_next,
    local_sem, send, recv,
):
    half = cols // 2
    chips = ny * nx
    zr = RANK // nz
    cr = RANK // chips
    y = lax.axis_index("dp")
    r = lax.axis_index("row")
    z = lax.axis_index("col")
    x = r // 2
    c = lax.rem(r, 2)

    def dev(dy=0, dx=0, dc=0, dz=0):
        return {
            "dp": lax.rem(y + dy, ny),
            "row": lax.rem(x + dx, nx) * 2 + lax.rem(c + dc, 2),
            "col": lax.rem(z + dz, nz),
        }

    def hops(d, n):
        return min(d, n - d)

    yz = [(dy, dz) for dz in range(nz) for dy in range(ny) if dy or dz]
    yz.sort(key=lambda d: -hops(d[0], ny) - hops(d[1], nz))
    plane = [(dy, dx) for dy in range(ny) for dx in range(nx) if dy or dx]
    plane.sort(key=lambda d: -hops(d[0], ny) - hops(d[1], nx))
    along_z = sorted(range(1, nz), key=lambda d: -hops(d, nz))
    zc = [(dz, dc) for dz in range(nz) for dc in range(2) if dz or dc]

    met = []
    for dy, dz in yz:
        met.append((dy, 0, 0, dz))
    for dy, dx in plane:
        if (dy, dx, 0, 0) not in met:
            met.append((dy, dx, 0, 0))
    for dz, dc in zc:
        if (0, 0, dc, dz) not in met:
            met.append((0, 0, dc, dz))
    loads = []
    for i, (src, dst) in enumerate([(right_hbm, right0), (grads.at[0], g_all), (mom_hbm, mom)]):
        copy = pltpu.make_async_copy(src, dst, local_sem.at[i])
        copy.start()
        loads.append(copy)
    barrier = pltpu.get_barrier_semaphore()
    for offsets in met:
        pl.semaphore_signal(barrier, inc=1, device_id=dev(*offsets), device_id_type=MESH)

    sent = []

    slots = {}

    def slot_of(name):
        return slots.setdefault(name, len(slots))

    def put(src, dst, name, target):
        slot = slot_of(name)
        pltpu.make_async_remote_copy(
            src_ref=src, dst_ref=dst, send_sem=send.at[slot], recv_sem=recv.at[slot],
            device_id=target, device_id_type=MESH,
        ).start()

    def landed(ref, name):
        slot = slot_of(name)
        copy = pltpu.make_async_remote_copy(
            src_ref=ref, dst_ref=ref, send_sem=send.at[slot], recv_sem=recv.at[slot],
            device_id=dev(), device_id_type=MESH,
        )
        copy.wait_recv()
        sent.append(copy)

    cuts = CUTS
    last = LAST
    hr = ROWS_DEV // 2

    def columns(k):
        first, size = cuts[k]
        return [pl.ds(first, size), pl.ds(half + first, size)]

    def part_rows(owner, start):
        return pl.ds(pl.multiple_of(owner * ROWS_DEV + start, hr), hr)

    after, opposite, before = lax.rem(y + 1, ny), lax.rem(y + 2, ny), lax.rem(y + 3, ny)

    def put_relay(k):
        for where in columns(k):
            put(g_all.at[part_rows(opposite, 0), where], g_relay.at[0, :, where], f"relay {k}", dev(1))
            put(g_all.at[part_rows(opposite, hr), where], g_relay.at[1, :, where], f"relay {k}", dev(3))

    def put_direct(k):
        for where in columns(k):
            put(g_all.at[part_rows(after, hr), where], g_direct.at[1, :, where], f"direct {k}", dev(1))
            put(g_all.at[part_rows(before, 0), where], g_direct.at[0, :, where], f"direct {k}", dev(3))

    def both_columns(ref, k):
        return ref.at[:, :, pl.ds(0, 2 * cuts[k][1])]

    def put_mixed(k):
        landed(both_columns(g_relay, k), f"relay {k}")
        for where in columns(k):
            for side, (owner, start, dy) in enumerate([(after, 0, 1), (before, hr, 3)]):
                own = g_all[part_rows(owner, start), where].astype(f32)
                g_mixed[side, :, where] = (own + g_relay[side, :, where].astype(f32)).astype(bf16)
                put(g_mixed.at[side, :, where], g_summed.at[side, :, where], f"summed {k}", dev(dy))

    def make_buffer(k):
        landed(both_columns(g_direct, k), f"direct {k}")
        landed(both_columns(g_summed, k), f"summed {k}")
        for where in columns(k):
            for side in range(2):
                rows = pl.ds(side * hr, hr)
                total = g_all[part_rows(y, side * hr), where].astype(f32)
                total = total + g_direct[side, :, where].astype(f32) + g_summed[side, :, where].astype(f32)
                buffer = (mom[rows, where].astype(f32) + total).astype(bf16)
                buf2[rows, where] = buffer
        first, size = cuts[k]
        ours = pl.ds(pl.multiple_of(c * half + first, 128), size)
        theirs = pl.ds(pl.multiple_of((1 - c) * half + first, 128), size)
        chip_buf[c, :, pl.ds(first, size)] = buf2[:, ours]
        put(buf2.at[:, theirs], chip_buf.at[c, :, pl.ds(first, size)], f"buffer {k}", dev(0, 0, 1))

    loads[0].wait()
    right_t = jnp.transpose(right0[...])
    loads[1].wait()
    for i in range(ny):
        if i == EARLY:
            pl.semaphore_wait(barrier, len(met))
            put_relay(0)
        p1_part[i] = nt(right_t, g_all[pl.ds(i * ROWS_DEV, ROWS_DEV), :])
    loads[2].wait()
    p1_part[y] = p1_part[y] + nt(right_t, mom[...])
    for i, (dy, dz) in enumerate(yz):
        there_y, there_z = lax.rem(y + dy, ny), lax.rem(z + dz, nz)
        put(
            p1_part.at[there_y, pl.ds(pl.multiple_of(there_z * zr, zr), zr), :], p1_recv.at[i],
            "power parts", dev(dy, 0, 0, dz),
        )
    put_relay(1)
    put_direct(0)
    put_relay(2)
    put_direct(1)
    put_mixed(0)
    put_direct(2)
    put_mixed(1)
    z_rows = pl.ds(pl.multiple_of(z * zr, zr), zr)

    def gather_z(step, slot):
        for dz in along_z:
            put(zbuf.at[step, z_rows, :], zbuf.at[step, z_rows, :], slot, dev(0, 0, 0, dz))

    landed(p1_recv, "power parts")
    total = p1_part[y, z_rows, :]
    for i in range(len(yz)):
        total = total + p1_recv[i]
    zbuf[0, z_rows, :] = total
    gather_z(0, "power 1")
    put_mixed(2)
    landed(z_recv, "power 1")

    mine = pl.ds(pl.multiple_of(c * half, 128), half)
    others = pl.ds(pl.multiple_of((1 - c) * half, 128), half)
    here = y * nx + x
    chip_rows = pl.ds(pl.multiple_of(here * cr, cr), cr)

    def to_plane(name, src, dst):
        for i, (dy, dx) in enumerate(plane):
            there = lax.rem(y + dy, ny) * nx + lax.rem(x + dx, nx)
            rows = pl.ds(pl.multiple_of(there * cr, cr), cr)
            put(src(rows), dst(i), name, dev(dy, dx))

    def reduce_plane(step, power):
        cuts = CUTS if step == 0 else LAST
        chip_power[step, c] = power
        put(chip_power.at[step, c], chip_power.at[step, c], f"power core {step}", dev(0, 0, 1))
        landed(chip_power.at[step, 0], f"power core {step}")
        power = jnp.concatenate([chip_power[step, 0], chip_power[step, 1]], 1)
        high, low = halves(power)

        def product(k):
            where = pl.ds(*cuts[k])
            rows = jnp.concatenate([chip_buf[0, :, where], chip_buf[1, :, where]], 0)
            m_own[step, :, where] = nn(high, rows) + nn(low, rows)

        def parts(k):
            where = pl.ds(*cuts[k])
            to_plane(
                f"back parts {step}{k}",
                lambda rows: m_own.at[step, rows, where], lambda i: m_slots.at[step, i, :, where],
            )

        def gram_parts():
            g_core[step] = nt(power, power, HIGHEST)
            to_plane(f"gram parts {step}", lambda rows: g_core.at[step, rows, :], lambda i: g_slots.at[step, i])

        for k in range(len(cuts)):
            if step == 0:
                make_buffer(k)
                if k == 0:
                    gram_parts()
                landed(chip_buf.at[0, :, pl.ds(*cuts[k])], f"buffer {k}")
            if step == 1 and k == 0:
                gram_parts()
            product(k)
            parts(k)
        landed(g_slots.at[step], f"gram parts {step}")
        total = g_core[step, chip_rows, :]
        for i in range(len(plane)):
            total = total + g_slots[step, i]
        g_full[step, chip_rows, :] = total
        for dy, dx in plane:
            put(g_full.at[step, chip_rows, :], g_full.at[step, chip_rows, :], f"gram {step}", dev(dy, dx))
        for k, (first, size) in enumerate(cuts):
            where = pl.ds(first, size)
            landed(m_slots.at[step, :, :, where], f"back parts {step}{k}")
            total = m_own[step, chip_rows, where]
            for i in range(len(plane)):
                total = total + m_slots[step, i, :, where]
            m_full[step, chip_rows, where] = total
            for dy, dx in plane:
                block = m_full.at[step, chip_rows, where]
                put(block, block, f"back {step}{k}", dev(dy, dx))

    def gram_done(step):
        landed(g_slots.at[step], f"gram {step}")
        return g_full[step]

    def back_done(step, k):
        landed(m_slots.at[step, :, :, pl.ds(*(cuts, last)[step][k])], f"back {step}{k}")

    reduce_plane(0, zbuf[0])
    next_part = jnp.zeros((2 * RANK, ROWS_DEV), f32)
    for k, (first, size) in enumerate(cuts):
        where = pl.ds(first, size)
        back_done(0, k)
        put(m_full.at[0, :, where], m_other.at[:, where], f"back other {k}", dev(0, 0, 1))
        both = jnp.concatenate(halves(m_full[0, :, where]), 0)
        next_part = next_part + nt(both, buf2[:, pl.ds(pl.multiple_of(c * half + first, 128), size)])
    for k, (first, size) in enumerate(cuts):
        where = pl.ds(first, size)
        landed(m_other.at[:, where], f"back other {k}")
        both = jnp.concatenate(halves(m_other[:, where]), 0)
        next_part = next_part + nt(both, buf2[:, pl.ds(pl.multiple_of((1 - c) * half + first, 128), size)])
    z_part[...] = next_part[:RANK] + next_part[RANK:]
    for dz in along_z:
        there = lax.rem(z + dz, nz)
        put(z_part.at[pl.ds(pl.multiple_of(there * zr, zr), zr), :], z_recv.at[dz - 1], "power 2 parts", dev(0, 0, 0, dz))
    w1 = inverse_cholesky(gram_done(0))
    landed(z_recv, "power 2 parts")
    total = z_part[z_rows, :]
    for i in range(nz - 1):
        total = total + z_recv[i]
    zbuf[1, z_rows, :] = total
    gather_z(1, "power 2")
    back_a = nn3(w1, m_full[0])
    back_b = nn3(w1, m_other[...])
    own_sum = jnp.sum(back_a * back_a, axis=1, keepdims=True) + jnp.sum(back_b * back_b, axis=1, keepdims=True)
    own_col = jnp.broadcast_to(own_sum, (RANK, RANK))
    own_row = jnp.transpose(own_col)
    n_mine[0] = own_row[0:8, :]
    for dz in along_z:
        put(n_mine.at[0], n1_recv.at[dz - 1], "norms 1", dev(0, 0, 0, dz))
    landed(z_recv, "power 2")

    power = nn(w1, zbuf[1], HIGHEST) * lax.rsqrt(own_col + 1e-6)
    reduce_plane(1, power)
    landed(n1_recv, "norms 1")
    norm = own_row[0:1, :]
    for i in range(nz - 1):
        norm = norm + n1_recv[i, 0:1, :]
    rest = jnp.sqrt((own_row[0:1, :] + 1e-6) / (norm + 1e-6))
    gram = gram_done(1) * column(rest) * rest
    w2 = inverse_cholesky(gram) * rest
    part = jnp.zeros((1, RANK), f32)
    for k, (first, size) in enumerate(last):
        where = pl.ds(first, size)
        back_done(1, k)
        back = jnp.transpose(nn3(w2, m_full[1, :, where]))
        part = part + jnp.sum(back * back, axis=0, keepdims=True)
        back_own[where, :] = back
    n_mine[1] = jnp.broadcast_to(part, (8, RANK))
    for i, (dz, dc) in enumerate(zc):
        put(n_mine.at[1], n2_recv.at[i], "norms 2", dev(0, 0, dc, dz))
    put(back_own, back_other, "last back", dev(0, 0, 1))
    basis = jnp.transpose(nn(w2, power, HIGHEST)).astype(bf16)
    mom_next[:, mine] = (
        buf2[:, mine].astype(f32) - 0.25 * nt(basis, back_own[...].astype(bf16))
    ).astype(bf16)
    basis_next[...] = basis
    landed(back_other, "last back")
    mom_next[:, others] = (
        buf2[:, others].astype(f32) - 0.25 * nt(basis, back_other[...].astype(bf16))
    ).astype(bf16)
    stores = [
        pltpu.make_async_copy(mom_next, mom_out, local_sem.at[3]),
        pltpu.make_async_copy(basis_next, basis_out, local_sem.at[4]),
        pltpu.make_async_copy(right_next, right_out, local_sem.at[5]),
    ]
    stores[0].start()
    stores[1].start()
    landed(n2_recv, "norms 2")
    norm = part
    for i in range(len(zc)):
        norm = norm + n2_recv[i, 0:1, :]
    scale = lax.rsqrt(norm + 1e-6)
    right_next[mine, :] = (back_own[...] * scale).astype(bf16)
    right_next[others, :] = (back_other[...] * scale).astype(bf16)
    stores[2].start()
    for copy in sent:
        copy.wait_send()
    for copy in stores:
        copy.wait()


def finish(factor, mom_in, right_in, basis_in, mom_out, right_out, upd_out, mom, right, basis, upd, sem):
    loads = [
        pltpu.make_async_copy(src, dst, sem.at[i])
        for i, (src, dst) in enumerate([(basis_in, basis), (right_in, right), (mom_in, mom)])
    ]
    for copy in loads:
        copy.start()
    stores = [pltpu.make_async_copy(right, right_out, sem.at[3]), pltpu.make_async_copy(mom, mom_out, sem.at[4])]
    loads[0].wait()
    loads[1].wait()
    stores[0].start()
    half = upd.shape[1] // 2
    for i in range(2):
        where = pl.ds(i * half, half)
        upd[:, where] = (factor * nt(basis[...], right[where, :])).astype(bf16)
        if i == 0:
            loads[2].wait()
            stores[1].start()
        stores.append(pltpu.make_async_copy(upd.at[:, where], upd_out.at[:, where], sem.at[5 + i]))
        stores[-1].start()
    for copy in stores:
        copy.wait()


def solution(mesh):
    ny, nx, nz = mesh.shape["dp"], mesh.shape["row"] // 2, mesh.shape["col"]

    def on_device(grad_parts, momentum, right_prev):
        cols = momentum.shape[1]
        half, chips = cols // 2, ny * nx
        zr, cr = RANK // nz, RANK // chips
        factor = math.sqrt(ny * nx * 2 * ROWS_DEV * cols * nz / RANK)
        vmem = pltpu.VMEM
        any_space = pl.BlockSpec(memory_space=pl.ANY)
        mom_shape = jax.ShapeDtypeStruct((ROWS_DEV, cols), bf16)
        right_shape = jax.ShapeDtypeStruct((cols, RANK), bf16)
        results = pl.pallas_call(
            functools.partial(kernel, ny, nx, nz, cols),
            out_shape=(mom_shape, right_shape, jax.ShapeDtypeStruct((ROWS_DEV, RANK), bf16)),
            in_specs=[any_space] * 3,
            out_specs=(any_space,) * 3,
            scratch_shapes=[
                vmem((ny * ROWS_DEV, cols), bf16),
                vmem((2, ROWS_DEV // 2, cols), bf16),
                vmem((2, ROWS_DEV // 2, cols), bf16),
                vmem((2, ROWS_DEV // 2, cols), bf16),
                vmem((2, ROWS_DEV // 2, cols), bf16),
                vmem((ROWS_DEV, cols), bf16),
                vmem((cols, RANK), bf16),
                vmem((ROWS_DEV, cols), bf16),
                vmem((ny, RANK, ROWS_DEV), f32),
                vmem((ny * nz - 1, zr, ROWS_DEV), f32),
                vmem((2, RANK, ROWS_DEV), f32),
                vmem((RANK, ROWS_DEV), f32),
                vmem((nz - 1, zr, ROWS_DEV), f32),
                vmem((2, ROWS_DEV, half), bf16),
                vmem((2, 2, RANK, ROWS_DEV), f32),
                vmem((2, RANK, half), f32),
                vmem((2, chips - 1, cr, half), f32),
                vmem((2, RANK, half), f32),
                vmem((RANK, half), f32),
                vmem((2, RANK, RANK), f32),
                vmem((2, chips - 1, cr, RANK), f32),
                vmem((2, RANK, RANK), f32),
                vmem((2, 8, RANK), f32),
                vmem((nz - 1, 8, RANK), f32),
                vmem((2 * nz - 1, 8, RANK), f32),
                vmem((half, RANK), f32),
                vmem((half, RANK), f32),
                vmem((ROWS_DEV, cols), bf16),
                vmem((cols, RANK), bf16),
                vmem((ROWS_DEV, RANK), bf16),
                pltpu.SemaphoreType.DMA((6,)),
                pltpu.SemaphoreType.DMA((48,)),
                pltpu.SemaphoreType.DMA((48,)),
            ],
            compiler_params=pltpu.CompilerParams(
                collective_id=0, has_side_effects=True, vmem_limit_bytes=VMEM_BYTES
            ),
            cost_estimate=pl.CostEstimate(flops=10**9, bytes_accessed=4 * 10**6, transcendentals=0),
        )(grad_parts, momentum, right_prev)
        return pl.pallas_call(
            functools.partial(finish, factor),
            out_shape=(mom_shape, right_shape, mom_shape),
            in_specs=[any_space] * 3,
            out_specs=(any_space,) * 3,
            scratch_shapes=[
                vmem((ROWS_DEV, cols), bf16),
                vmem((cols, RANK), bf16),
                vmem((ROWS_DEV, RANK), bf16),
                vmem((ROWS_DEV, cols), bf16),
                pltpu.SemaphoreType.DMA((7,)),
            ],
            compiler_params=pltpu.CompilerParams(vmem_limit_bytes=VMEM_BYTES),
            cost_estimate=pl.CostEstimate(flops=6 * 10**7, bytes_accessed=3 * 10**6, transcendentals=0),
        )(*results)

    return jax.shard_map(
        on_device,
        mesh=mesh,
        in_specs=(P("dp", "row", "col"), P(("row", "dp"), "col"), P("col", None)),
        out_specs=(P(("row", "dp"), "col"), P("col", None), P(("row", "dp"), "col")),
        check_vma=False,
    )
```

```python
import functools
import math

import jax
import jax.numpy as jnp
from jax import lax
from jax.experimental import pallas as pl
from jax.experimental.pallas import tpu as pltpu
from jax.sharding import PartitionSpec as P

f32 = jnp.float32
bf16 = jnp.bfloat16
HIGHEST = lax.Precision.HIGHEST
MESH = pl.DeviceIdType.MESH
RANK = 128
ROWS_DEV = 128
PANEL = 8
VMEM_BYTES = 63 * 1024 * 1024
CUTS = [(0, 384), (384, 256), (640, 256)]
LAST = [(0, 384), (384, 256), (640, 256)]
EARLY = 2


def nt(a, b, precision=None):
    return lax.dot_general(a, b, (((1,), (1,)), ((), ())), precision=precision, preferred_element_type=f32)


def nn(a, b, precision=None):
    return lax.dot_general(a, b, (((1,), (0,)), ((), ())), precision=precision, preferred_element_type=f32)


def halves(x):
    high = x.astype(bf16)
    return high, (x - high.astype(f32)).astype(bf16)


def nn3(a, b):
    a_high, a_low = halves(a)
    b_high, b_low = halves(b)
    return nn(a_high, b_high) + (nn(a_high, b_low) + nn(a_low, b_high))


def inverse_cholesky(a, ahead=2):
    n, count = RANK, RANK // PANEL
    rows = [a[PANEL * i : PANEL * (i + 1), :] for i in range(count)]
    row = lax.broadcasted_iota(jnp.int32, (PANEL, n), 0)
    lane = lax.broadcasted_iota(jnp.int32, (PANEL, n), 1)
    inv = [(lane == row + PANEL * i).astype(f32) for i in range(count)]
    out = []
    for b in range(count):
        end = min(count, b + 1 + ahead)
        cols = [
            [jnp.broadcast_to(rows[i][:, PANEL * b + k : PANEL * b + k + 1], (PANEL, n)) for k in range(PANEL)]
            for i in range(b, end)
        ]
        recips = []
        for j in range(PANEL):
            recip = 1.0 / jnp.broadcast_to(cols[0][j][j : j + 1, :], (PANEL, n))
            recips.append(recip)
            pivots = [jnp.broadcast_to(cols[0][k][j : j + 1, :], (PANEL, n)) for k in range(j + 1, PANEL)]
            row_a = jnp.broadcast_to(rows[b][j : j + 1, :], (PANEL, n))
            row_w = jnp.broadcast_to(inv[b][j : j + 1, :], (PANEL, n))
            for i in range(b, end):
                m = cols[i - b][j] * recip
                if i == b:
                    m = jnp.where(row > j, m, 0.0)
                for k in range(j + 1, PANEL):
                    cols[i - b][k] = cols[i - b][k] - m * pivots[k - j - 1]
                rows[i] = rows[i] - m * row_a
                inv[i] = inv[i] - m * row_w
        scale = recips[0]
        for j in range(1, PANEL):
            scale = jnp.where(row == j, recips[j], scale)
        out.append(inv[b] * jnp.sqrt(scale))
        if end < count:
            left = jnp.transpose(rows[b] * scale)[PANEL * end :, :]
            update = nn(left, jnp.concatenate([rows[b], inv[b]], 1), HIGHEST)
            for i in range(end, count):
                part = update[PANEL * (i - end) : PANEL * (i - end + 1), :]
                rows[i] = rows[i] - part[:, :n]
                inv[i] = inv[i] - part[:, n:]
    return jnp.concatenate(out, 0)


def column(row):
    return jnp.transpose(jnp.broadcast_to(row, (RANK, RANK)))


def kernel(
    ny, nx, nz, cols,
    grads, mom_hbm, right_hbm,
    mom_out, right_out, basis_out,
    g_all, g_relay, g_direct, g_mixed, g_summed, mom, right0, buf2,
    p1_part, p1_recv, zbuf, z_part, z_recv,
    chip_buf, chip_power, m_own, m_slots, m_full, m_other,
    g_core, g_slots, g_full,
    n_mine, n1_recv, n2_recv, back_own, back_other, mom_next, right_next, basis_next,
    local_sem, send, recv,
):
    half = cols // 2
    chips = ny * nx
    zr = RANK // nz
    cr = RANK // chips
    y = lax.axis_index("dp")
    r = lax.axis_index("row")
    z = lax.axis_index("col")
    x = r // 2
    c = lax.rem(r, 2)

    def dev(dy=0, dx=0, dc=0, dz=0):
        return {
            "dp": lax.rem(y + dy, ny),
            "row": lax.rem(x + dx, nx) * 2 + lax.rem(c + dc, 2),
            "col": lax.rem(z + dz, nz),
        }

    def hops(d, n):
        return min(d, n - d)

    yz = [(dy, dz) for dz in range(nz) for dy in range(ny) if dy or dz]
    yz.sort(key=lambda d: -hops(d[0], ny) - hops(d[1], nz))
    plane = [(dy, dx) for dy in range(ny) for dx in range(nx) if dy or dx]
    plane.sort(key=lambda d: (-hops(d[0], ny), -hops(d[1], nx)))
    along_z = sorted(range(1, nz), key=lambda d: -hops(d, nz))
    zc = [(dz, dc) for dz in range(nz) for dc in range(2) if dz or dc]

    met = []
    for dy, dz in yz:
        met.append((dy, 0, 0, dz))
    for dy, dx in plane:
        if (dy, dx, 0, 0) not in met:
            met.append((dy, dx, 0, 0))
    for dz, dc in zc:
        if (0, 0, dc, dz) not in met:
            met.append((0, 0, dc, dz))
    loads = []
    for i, (src, dst) in enumerate([(right_hbm, right0), (grads.at[0], g_all), (mom_hbm, mom)]):
        copy = pltpu.make_async_copy(src, dst, local_sem.at[i])
        copy.start()
        loads.append(copy)
    barrier = pltpu.get_barrier_semaphore()
    for offsets in met:
        pl.semaphore_signal(barrier, inc=1, device_id=dev(*offsets), device_id_type=MESH)

    sent = []

    slots = {}

    def slot_of(name):
        return slots.setdefault(name, len(slots))

    def put(src, dst, name, target):
        slot = slot_of(name)
        pltpu.make_async_remote_copy(
            src_ref=src, dst_ref=dst, send_sem=send.at[slot], recv_sem=recv.at[slot],
            device_id=target, device_id_type=MESH,
        ).start()

    def landed(ref, name):
        slot = slot_of(name)
        copy = pltpu.make_async_remote_copy(
            src_ref=ref, dst_ref=ref, send_sem=send.at[slot], recv_sem=recv.at[slot],
            device_id=dev(), device_id_type=MESH,
        )
        copy.wait_recv()
        sent.append(copy)

    cuts = CUTS
    last = LAST
    hr = ROWS_DEV // 2

    def columns(k):
        first, size = cuts[k]
        return [pl.ds(first, size), pl.ds(half + first, size)]

    def part_rows(owner, start):
        return pl.ds(pl.multiple_of(owner * ROWS_DEV + start, hr), hr)

    after, opposite, before = lax.rem(y + 1, ny), lax.rem(y + 2, ny), lax.rem(y + 3, ny)

    def put_relay(k):
        for where in columns(k):
            put(g_all.at[part_rows(opposite, 0), where], g_relay.at[0, :, where], f"relay {k}", dev(1))
            put(g_all.at[part_rows(opposite, hr), where], g_relay.at[1, :, where], f"relay {k}", dev(3))

    def put_direct(k):
        for where in columns(k):
            put(g_all.at[part_rows(after, hr), where], g_direct.at[1, :, where], f"direct {k}", dev(1))
            put(g_all.at[part_rows(before, 0), where], g_direct.at[0, :, where], f"direct {k}", dev(3))

    def both_columns(ref, k):
        return ref.at[:, :, pl.ds(0, 2 * cuts[k][1])]

    def put_mixed(k):
        landed(both_columns(g_relay, k), f"relay {k}")
        for where in columns(k):
            for side, (owner, start, dy) in enumerate([(after, 0, 1), (before, hr, 3)]):
                own = g_all[part_rows(owner, start), where].astype(f32)
                g_mixed[side, :, where] = (own + g_relay[side, :, where].astype(f32)).astype(bf16)
                put(g_mixed.at[side, :, where], g_summed.at[side, :, where], f"summed {k}", dev(dy))

    def make_buffer(k):
        landed(both_columns(g_direct, k), f"direct {k}")
        landed(both_columns(g_summed, k), f"summed {k}")
        for where in columns(k):
            for side in range(2):
                rows = pl.ds(side * hr, hr)
                total = g_all[part_rows(y, side * hr), where].astype(f32)
                total = total + g_direct[side, :, where].astype(f32) + g_summed[side, :, where].astype(f32)
                buffer = (mom[rows, where].astype(f32) + total).astype(bf16)
                buf2[rows, where] = buffer
        first, size = cuts[k]
        ours = pl.ds(pl.multiple_of(c * half + first, 128), size)
        theirs = pl.ds(pl.multiple_of((1 - c) * half + first, 128), size)
        chip_buf[c, :, pl.ds(first, size)] = buf2[:, ours]
        put(buf2.at[:, theirs], chip_buf.at[c, :, pl.ds(first, size)], f"buffer {k}", dev(0, 0, 1))

    loads[0].wait()
    right_t = jnp.transpose(right0[...])
    loads[1].wait()
    for i in range(ny):
        if i == EARLY:
            pl.semaphore_wait(barrier, len(met))
            put_relay(0)
        p1_part[i] = nt(right_t, g_all[pl.ds(i * ROWS_DEV, ROWS_DEV), :])
    loads[2].wait()
    p1_part[y] = p1_part[y] + nt(right_t, mom[...])
    for i, (dy, dz) in enumerate(yz):
        there_y, there_z = lax.rem(y + dy, ny), lax.rem(z + dz, nz)
        put(
            p1_part.at[there_y, pl.ds(pl.multiple_of(there_z * zr, zr), zr), :], p1_recv.at[i],
            "power parts", dev(dy, 0, 0, dz),
        )
    put_relay(1)
    put_direct(0)
    put_relay(2)
    put_direct(1)
    put_mixed(0)
    put_direct(2)
    put_mixed(1)
    z_rows = pl.ds(pl.multiple_of(z * zr, zr), zr)

    def gather_z(step, slot):
        for dz in along_z:
            put(zbuf.at[step, z_rows, :], zbuf.at[step, z_rows, :], slot, dev(0, 0, 0, dz))

    landed(p1_recv, "power parts")
    total = p1_part[y, z_rows, :]
    for i in range(len(yz)):
        total = total + p1_recv[i]
    zbuf[0, z_rows, :] = total
    gather_z(0, "power 1")
    put_mixed(2)
    landed(z_recv, "power 1")

    mine = pl.ds(pl.multiple_of(c * half, 128), half)
    others = pl.ds(pl.multiple_of((1 - c) * half, 128), half)
    here = y * nx + x
    chip_rows = pl.ds(pl.multiple_of(here * cr, cr), cr)

    def to_plane(name, src, dst):
        for i, (dy, dx) in enumerate(plane):
            there = lax.rem(y + dy, ny) * nx + lax.rem(x + dx, nx)
            rows = pl.ds(pl.multiple_of(there * cr, cr), cr)
            put(src(rows), dst(i), name, dev(dy, dx))

    def reduce_plane(step, power):
        cuts = CUTS if step == 0 else LAST
        chip_power[step, c] = power
        put(chip_power.at[step, c], chip_power.at[step, c], f"power core {step}", dev(0, 0, 1))
        landed(chip_power.at[step, 0], f"power core {step}")
        power = jnp.concatenate([chip_power[step, 0], chip_power[step, 1]], 1)
        high, low = halves(power)

        def product(k):
            where = pl.ds(*cuts[k])
            rows = jnp.concatenate([chip_buf[0, :, where], chip_buf[1, :, where]], 0)
            m_own[step, :, where] = nn(high, rows) + nn(low, rows)

        def parts(k):
            where = pl.ds(*cuts[k])
            to_plane(
                f"back parts {step}{k}",
                lambda rows: m_own.at[step, rows, where], lambda i: m_slots.at[step, i, :, where],
            )

        def gram_parts():
            g_core[step] = nt(power, power, HIGHEST)
            to_plane(f"gram parts {step}", lambda rows: g_core.at[step, rows, :], lambda i: g_slots.at[step, i])

        for k in range(len(cuts)):
            if step == 0:
                make_buffer(k)
                if k == 0:
                    gram_parts()
                landed(chip_buf.at[0, :, pl.ds(*cuts[k])], f"buffer {k}")
            if step == 1 and k == 0:
                gram_parts()
            product(k)
            parts(k)
        landed(g_slots.at[step], f"gram parts {step}")
        total = g_core[step, chip_rows, :]
        for i in range(len(plane)):
            total = total + g_slots[step, i]
        g_full[step, chip_rows, :] = total
        for dy, dx in plane:
            put(g_full.at[step, chip_rows, :], g_full.at[step, chip_rows, :], f"gram {step}", dev(dy, dx))
        for k, (first, size) in enumerate(cuts):
            where = pl.ds(first, size)
            landed(m_slots.at[step, :, :, where], f"back parts {step}{k}")
            total = m_own[step, chip_rows, where]
            for i in range(len(plane)):
                total = total + m_slots[step, i, :, where]
            m_full[step, chip_rows, where] = total
            for dy, dx in plane:
                block = m_full.at[step, chip_rows, where]
                put(block, block, f"back {step}{k}", dev(dy, dx))

    def gram_done(step):
        landed(g_slots.at[step], f"gram {step}")
        return g_full[step]

    def back_done(step, k):
        landed(m_slots.at[step, :, :, pl.ds(*(cuts, last)[step][k])], f"back {step}{k}")

    reduce_plane(0, zbuf[0])
    next_part = jnp.zeros((2 * RANK, ROWS_DEV), f32)
    for k, (first, size) in enumerate(cuts):
        where = pl.ds(first, size)
        back_done(0, k)
        put(m_full.at[0, :, where], m_other.at[:, where], f"back other {k}", dev(0, 0, 1))
        both = jnp.concatenate(halves(m_full[0, :, where]), 0)
        next_part = next_part + nt(both, buf2[:, pl.ds(pl.multiple_of(c * half + first, 128), size)])
    for k, (first, size) in enumerate(cuts):
        where = pl.ds(first, size)
        landed(m_other.at[:, where], f"back other {k}")
        both = jnp.concatenate(halves(m_other[:, where]), 0)
        next_part = next_part + nt(both, buf2[:, pl.ds(pl.multiple_of((1 - c) * half + first, 128), size)])
    z_part[...] = next_part[:RANK] + next_part[RANK:]
    for dz in along_z:
        there = lax.rem(z + dz, nz)
        put(z_part.at[pl.ds(pl.multiple_of(there * zr, zr), zr), :], z_recv.at[dz - 1], "power 2 parts", dev(0, 0, 0, dz))
    w1 = inverse_cholesky(gram_done(0))
    landed(z_recv, "power 2 parts")
    total = z_part[z_rows, :]
    for i in range(nz - 1):
        total = total + z_recv[i]
    zbuf[1, z_rows, :] = total
    gather_z(1, "power 2")
    back_a = nn3(w1, m_full[0])
    back_b = nn3(w1, m_other[...])
    own_sum = jnp.sum(back_a * back_a, axis=1, keepdims=True) + jnp.sum(back_b * back_b, axis=1, keepdims=True)
    own_col = jnp.broadcast_to(own_sum, (RANK, RANK))
    own_row = jnp.transpose(own_col)
    n_mine[0] = own_row[0:8, :]
    for dz in along_z:
        put(n_mine.at[0], n1_recv.at[dz - 1], "norms 1", dev(0, 0, 0, dz))
    landed(z_recv, "power 2")

    power = nn(w1, zbuf[1], HIGHEST) * lax.rsqrt(own_col + 1e-6)
    reduce_plane(1, power)
    landed(n1_recv, "norms 1")
    norm = own_row[0:1, :]
    for i in range(nz - 1):
        norm = norm + n1_recv[i, 0:1, :]
    rest = jnp.sqrt((own_row[0:1, :] + 1e-6) / (norm + 1e-6))
    gram = gram_done(1) * column(rest) * rest
    w2 = inverse_cholesky(gram) * rest
    part = jnp.zeros((1, RANK), f32)
    for k, (first, size) in enumerate(last):
        where = pl.ds(first, size)
        back_done(1, k)
        back = jnp.transpose(nn3(w2, m_full[1, :, where]))
        part = part + jnp.sum(back * back, axis=0, keepdims=True)
        back_own[where, :] = back
    n_mine[1] = jnp.broadcast_to(part, (8, RANK))
    for i, (dz, dc) in enumerate(zc):
        put(n_mine.at[1], n2_recv.at[i], "norms 2", dev(0, 0, dc, dz))
    put(back_own, back_other, "last back", dev(0, 0, 1))
    basis = jnp.transpose(nn(w2, power, HIGHEST)).astype(bf16)
    mom_next[:, mine] = (
        buf2[:, mine].astype(f32) - 0.25 * nt(basis, back_own[...].astype(bf16))
    ).astype(bf16)
    basis_next[...] = basis
    landed(back_other, "last back")
    mom_next[:, others] = (
        buf2[:, others].astype(f32) - 0.25 * nt(basis, back_other[...].astype(bf16))
    ).astype(bf16)
    stores = [
        pltpu.make_async_copy(mom_next, mom_out, local_sem.at[3]),
        pltpu.make_async_copy(basis_next, basis_out, local_sem.at[4]),
        pltpu.make_async_copy(right_next, right_out, local_sem.at[5]),
    ]
    stores[0].start()
    stores[1].start()
    landed(n2_recv, "norms 2")
    norm = part
    for i in range(len(zc)):
        norm = norm + n2_recv[i, 0:1, :]
    scale = lax.rsqrt(norm + 1e-6)
    right_next[mine, :] = (back_own[...] * scale).astype(bf16)
    right_next[others, :] = (back_other[...] * scale).astype(bf16)
    stores[2].start()
    for copy in sent:
        copy.wait_send()
    for copy in stores:
        copy.wait()


def finish(factor, mom_in, right_in, basis_in, mom_out, right_out, upd_out, mom, right, basis, upd, sem):
    loads = [
        pltpu.make_async_copy(src, dst, sem.at[i])
        for i, (src, dst) in enumerate([(basis_in, basis), (right_in, right), (mom_in, mom)])
    ]
    for copy in loads:
        copy.start()
    stores = [pltpu.make_async_copy(right, right_out, sem.at[3]), pltpu.make_async_copy(mom, mom_out, sem.at[4])]
    loads[0].wait()
    loads[1].wait()
    stores[0].start()
    half = upd.shape[1] // 2
    for i in range(2):
        where = pl.ds(i * half, half)
        upd[:, where] = (factor * nt(basis[...], right[where, :])).astype(bf16)
        if i == 0:
            loads[2].wait()
            stores[1].start()
        stores.append(pltpu.make_async_copy(upd.at[:, where], upd_out.at[:, where], sem.at[5 + i]))
        stores[-1].start()
    for copy in stores:
        copy.wait()


def solution(mesh):
    ny, nx, nz = mesh.shape["dp"], mesh.shape["row"] // 2, mesh.shape["col"]

    def on_device(grad_parts, momentum, right_prev):
        cols = momentum.shape[1]
        half, chips = cols // 2, ny * nx
        zr, cr = RANK // nz, RANK // chips
        factor = math.sqrt(ny * nx * 2 * ROWS_DEV * cols * nz / RANK)
        vmem = pltpu.VMEM
        any_space = pl.BlockSpec(memory_space=pl.ANY)
        mom_shape = jax.ShapeDtypeStruct((ROWS_DEV, cols), bf16)
        right_shape = jax.ShapeDtypeStruct((cols, RANK), bf16)
        results = pl.pallas_call(
            functools.partial(kernel, ny, nx, nz, cols),
            out_shape=(mom_shape, right_shape, jax.ShapeDtypeStruct((ROWS_DEV, RANK), bf16)),
            in_specs=[any_space] * 3,
            out_specs=(any_space,) * 3,
            scratch_shapes=[
                vmem((ny * ROWS_DEV, cols), bf16),
                vmem((2, ROWS_DEV // 2, cols), bf16),
                vmem((2, ROWS_DEV // 2, cols), bf16),
                vmem((2, ROWS_DEV // 2, cols), bf16),
                vmem((2, ROWS_DEV // 2, cols), bf16),
                vmem((ROWS_DEV, cols), bf16),
                vmem((cols, RANK), bf16),
                vmem((ROWS_DEV, cols), bf16),
                vmem((ny, RANK, ROWS_DEV), f32),
                vmem((ny * nz - 1, zr, ROWS_DEV), f32),
                vmem((2, RANK, ROWS_DEV), f32),
                vmem((RANK, ROWS_DEV), f32),
                vmem((nz - 1, zr, ROWS_DEV), f32),
                vmem((2, ROWS_DEV, half), bf16),
                vmem((2, 2, RANK, ROWS_DEV), f32),
                vmem((2, RANK, half), f32),
                vmem((2, chips - 1, cr, half), f32),
                vmem((2, RANK, half), f32),
                vmem((RANK, half), f32),
                vmem((2, RANK, RANK), f32),
                vmem((2, chips - 1, cr, RANK), f32),
                vmem((2, RANK, RANK), f32),
                vmem((2, 8, RANK), f32),
                vmem((nz - 1, 8, RANK), f32),
                vmem((2 * nz - 1, 8, RANK), f32),
                vmem((half, RANK), f32),
                vmem((half, RANK), f32),
                vmem((ROWS_DEV, cols), bf16),
                vmem((cols, RANK), bf16),
                vmem((ROWS_DEV, RANK), bf16),
                pltpu.SemaphoreType.DMA((6,)),
                pltpu.SemaphoreType.DMA((48,)),
                pltpu.SemaphoreType.DMA((48,)),
            ],
            compiler_params=pltpu.CompilerParams(
                collective_id=0, has_side_effects=True, vmem_limit_bytes=VMEM_BYTES
            ),
            cost_estimate=pl.CostEstimate(flops=10**9, bytes_accessed=4 * 10**6, transcendentals=0),
        )(grad_parts, momentum, right_prev)
        return pl.pallas_call(
            functools.partial(finish, factor),
            out_shape=(mom_shape, right_shape, mom_shape),
            in_specs=[any_space] * 3,
            out_specs=(any_space,) * 3,
            scratch_shapes=[
                vmem((ROWS_DEV, cols), bf16),
                vmem((cols, RANK), bf16),
                vmem((ROWS_DEV, RANK), bf16),
                vmem((ROWS_DEV, cols), bf16),
                pltpu.SemaphoreType.DMA((7,)),
            ],
            compiler_params=pltpu.CompilerParams(vmem_limit_bytes=VMEM_BYTES),
            cost_estimate=pl.CostEstimate(flops=6 * 10**7, bytes_accessed=3 * 10**6, transcendentals=0),
        )(*results)

    return jax.shard_map(
        on_device,
        mesh=mesh,
        in_specs=(P("dp", "row", "col"), P(("row", "dp"), "col"), P("col", None)),
        out_specs=(P(("row", "dp"), "col"), P("col", None), P(("row", "dp"), "col")),
        check_vma=False,
    )
```
